32 devices in a mesh: wide: 16 (over z, x, core), narrow: 2 (over y).
Axes of the slice: x: 2, y: 2, z: 4, core: 2. Of those that a mesh axis runs over, the one named last changes fastest.
Arguments:
- patches: bfloat16 [16, 256, 1280], P('wide', None, 'narrow'), may hold values from -8 to 8
- grid: int32 [16, 2], P('wide'), may hold values from 2 to 16, as said below
- vit_gain: float32 [1280], replicated, may hold values from 0.25 to 1.75
- vit_qkv: bfloat16 [1280, 3840], P('wide', 'narrow'), may hold values from -1 to 1
- vit_out: bfloat16 [1280, 1280], P('narrow', 'wide'), may hold values from -0.625 to 0.625
- merge_weight: bfloat16 [4, 1280, 1280], P(None, 'narrow', 'wide'), may hold values from -0.078125 to 0.078125
- text_embeds: bfloat16 [2560, 1280], P('wide', 'narrow'), may hold values from -8 to 8
- prompt_pos: int32 [16, 64], replicated, may hold values from -1 to 2559, as said below
- dec_gain: float32 [1280], replicated, may hold values from 0.25 to 1.75
- dec_qkv: bfloat16 [1280, 3840], P('wide', 'narrow'), may hold values from -1 to 1
- dec_out: bfloat16 [1280, 1280], P('narrow', 'wide'), may hold values from -1.25 to 1.25
Outputs:
- decoded: bfloat16 [2560, 1280], P('wide', 'narrow')
The draws below stay inside these ranges and needn't reach their ends.
Inputs may be any that keep to these rules, and one draw needn't show every extreme that they name: `prompt_pos`: grid entries are even; a merged slot (r, c) is live when 2r < grid rows and 2c < grid columns; live slots carry distinct positions, one image's live slots being consecutive in row-major order, and padded slots carry -1. `grid`: patch rows and columns of an image are even.
All inputs are finite; a program needn't handle non-finite values.
Results may differ from the reference program's by a relative error of at most 0.02.
Values may be sent and summed in bfloat16 or wider, within the bound.
No kernel may reach another device: no remote copies, remote signals or barrier semaphores. Data moves between devices by JAX's collectives and lax.ppermute only.
A program may use at most 64 MiB of HBM per device.

```python
import math
import jax
import jax.numpy as jnp
from jax import lax

D = 1280
HEADS = 16
HEAD = 80
PATCH_SIDE = 16
SLOTS = 256
MERGED = 64
IMAGES = 16
SEQ = 2560


def layout_helper(key):
    base = jax.random.fold_in(key, 17)
    key_rows = jax.random.fold_in(base, 1)
    key_cols = jax.random.fold_in(base, 2)
    side_half = PATCH_SIDE // 2
    heights = 2 * jax.random.randint(key_rows, (IMAGES,), 1, side_half + 1)
    widths = 2 * jax.random.randint(key_cols, (IMAGES,), 1, side_half + 1)
    return (heights.astype(jnp.int32), widths.astype(jnp.int32))


def draw_grid(key, part):
    heights, widths = layout_helper(key)
    return jnp.stack([heights, widths], axis=1).astype(jnp.int32)


def draw_prompt_pos(key, part):
    heights, widths = layout_helper(key)
    half_side = PATCH_SIDE // 2
    rows_merged = heights // 2
    cols_merged = widths // 2
    counts = (rows_merged * cols_merged).astype(jnp.int32)
    order_key = jax.random.fold_in(key, 29)
    gap_key = jax.random.fold_in(key, 31)
    order = jax.random.permutation(order_key, IMAGES).astype(jnp.int32)
    rank = jnp.argsort(order, stable=True).astype(jnp.int32)
    free_rows = (SEQ - jnp.sum(counts)).astype(jnp.int32)
    gaps = jax.random.randint(gap_key, (IMAGES,), 1, 8).astype(jnp.int32)
    cumulative = jnp.cumsum(gaps).astype(jnp.int32)
    bounds = (free_rows * cumulative // cumulative[IMAGES - 1]).astype(jnp.int32)
    earlier = jnp.sum(jnp.where(rank[None, :] < rank[:, None], counts[None, :], 0), axis=1).astype(jnp.int32)
    start = bounds[rank] + earlier
    slot = jnp.arange(half_side * half_side, dtype=jnp.int32)
    row_index = slot // half_side
    col_index = slot % half_side
    live = (row_index[None, :] < rows_merged[:, None]) & (col_index[None, :] < cols_merged[:, None])
    placed = start[:, None] + row_index[None, :] * cols_merged[:, None] + col_index[None, :]
    return jnp.where(live, placed, -1).astype(jnp.int32)


def drawn_normal(key, tag, shape):
    return jnp.clip(jax.random.normal(jax.random.fold_in(key, tag), shape, jnp.float32), -6.0, 6.0)


def draw_patches(key, part):
    values = drawn_normal(key, 41, (IMAGES, SLOTS, D))
    return values.astype(jnp.bfloat16)


def draw_vit_qkv(key, part):
    values = drawn_normal(key, 71, (D, HEADS, 3, HEAD)) * D ** (-0.5)
    return values.reshape(D, 3 * D).astype(jnp.bfloat16)


def draw_text_embeds(key, part):
    values = drawn_normal(key, 53, (SEQ, D))
    return values.astype(jnp.bfloat16)


def draw_dec_qkv(key, part):
    values = drawn_normal(key, 79, (D, HEADS, 3, HEAD)) * D ** (-0.5)
    return values.reshape(D, 3 * D).astype(jnp.bfloat16)


def steps_of(key, extent, shards, low, largest):
    level, own = 1.0, jax.random.fold_in(key, 6)
    for position, shards_of in shards:
        steps = jnp.exp(jax.random.uniform(jax.random.fold_in(own, position), (shards_of,), jnp.float32, low / len(shards), largest / len(shards)))
        level = level * jnp.repeat(steps, extent[position] // shards_of).reshape([-1 if axis == position else 1 for axis in range(len(extent))])
    return level


def gaussian(rng, extent, scale, bound, shards=(), held_as=jnp.bfloat16):
    entries = jax.random.normal(rng, extent, jnp.float32) * scale
    if len(shards) > 0:
        entries = steps_of(rng, extent, shards, -0.22, 0.18) * entries
    return jnp.clip(entries, min=-bound, max=bound).astype(held_as)


def setup_inputs(seed: int = 0) -> dict:
    key_of = jax.random.split(jax.random.key(seed), 12)
    patches = draw_patches(jax.random.fold_in(key_of[11], 71), 0)
    grid = draw_grid(jax.random.fold_in(key_of[11], 71), 0)
    vit_gain = jnp.clip(1.0 + 0.15 * jax.random.normal(key_of[2], (D,), jnp.float32), 0.25, 1.75)
    vit_qkv = draw_vit_qkv(jax.random.fold_in(key_of[11], 71), 0)
    vit_out = gaussian(key_of[4], (D, D), (D // 16) ** -0.5, 0.625, ((0, 2), (1, 16)))
    merge_weight = gaussian(key_of[5], (4, D, D), (4 * D) ** -0.5, 0.078125, ((1, 2), (2, 16)))
    text_embeds = draw_text_embeds(jax.random.fold_in(key_of[11], 71), 0)
    prompt_pos = draw_prompt_pos(jax.random.fold_in(key_of[11], 71), 0)
    dec_gain = jnp.clip(1.0 + 0.15 * jax.random.normal(key_of[8], (D,), jnp.float32), 0.25, 1.75)
    dec_qkv = draw_dec_qkv(jax.random.fold_in(key_of[11], 71), 0)
    dec_out = gaussian(key_of[10], (D, D), (D // 64) ** -0.5, 1.25, ((0, 2), (1, 16)))
    return {"patches": patches, "grid": grid, "vit_gain": vit_gain, "vit_qkv": vit_qkv, "vit_out": vit_out, "merge_weight": merge_weight, "text_embeds": text_embeds, "prompt_pos": prompt_pos, "dec_gain": dec_gain, "dec_qkv": dec_qkv, "dec_out": dec_out}


eps_norm = 1e-06

def layer_norm(values, gain):
    center = values - lax.optimization_barrier(jnp.mean(values, axis=-1, keepdims=True))
    spread = lax.optimization_barrier(jnp.mean(center * center, axis=-1, keepdims=True))
    return center * lax.rsqrt(spread + eps_norm) * gain

def rms_norm(values, gain):
    return values * lax.rsqrt(lax.optimization_barrier(jnp.mean(values * values, axis=-1, keepdims=True)) + eps_norm) * gain

def image_attention(inputs):
    query, keys, values, keep = inputs
    scores = jnp.einsum('qhd,khd->hqk', query.astype(jnp.float32), keys.astype(jnp.float32)) * HEAD ** (-0.5)
    scores = jnp.where(keep[None, None, :], scores, -jnp.inf)
    weights = jnp.exp(scores - lax.optimization_barrier(jnp.max(scores, axis=-1, keepdims=True)))
    total = lax.optimization_barrier(jnp.sum(weights, axis=-1))
    mixed = jnp.einsum('hqk,khd->qhd', weights.astype(jnp.bfloat16).astype(jnp.float32), values.astype(jnp.float32))
    mixed = mixed / jnp.transpose(total, (1, 0))[..., None]
    return mixed.astype(jnp.bfloat16).reshape(SLOTS, D)

def reference(patches, grid, vit_gain, vit_qkv, vit_out, merge_weight, text_embeds, prompt_pos, dec_gain, dec_qkv, dec_out):
    side = PATCH_SIDE
    half_side = side // 2
    slot_ids = jnp.arange(SLOTS, dtype=jnp.int32)
    keep = ((slot_ids // side)[None, :] < grid[:, 0:1]) & ((slot_ids % side)[None, :] < grid[:, 1:2])
    normed = layer_norm(patches.astype(jnp.float32), vit_gain).astype(jnp.bfloat16)
    projected = jnp.dot(normed.reshape(IMAGES * SLOTS, D), vit_qkv, preferred_element_type=jnp.float32)
    projected = projected.astype(jnp.bfloat16).reshape(IMAGES, SLOTS, HEADS, 3, HEAD)
    attended = lax.map(image_attention, (projected[:, :, :, 0], projected[:, :, :, 1], projected[:, :, :, 2], keep))
    branch = jnp.dot(attended.reshape(IMAGES * SLOTS, D), vit_out, preferred_element_type=jnp.float32)
    after = (patches.reshape(IMAGES * SLOTS, D).astype(jnp.float32) + branch).astype(jnp.bfloat16)
    grouped = after.reshape(IMAGES, half_side, 2, half_side, 2, D).transpose(0, 1, 3, 2, 4, 5)
    grouped = grouped.reshape(IMAGES * MERGED, 4 * D)
    merged = jnp.dot(grouped, merge_weight.reshape(4 * D, D), preferred_element_type=jnp.float32).astype(jnp.bfloat16)
    flat_pos = prompt_pos.reshape(-1)
    target = jnp.where(flat_pos < 0, SEQ, flat_pos).astype(jnp.int32)
    dec_in = text_embeds.at[target].set(merged, mode='drop')
    dec_normed = rms_norm(dec_in.astype(jnp.float32), dec_gain).astype(jnp.bfloat16)
    dec_proj = jnp.dot(dec_normed, dec_qkv, preferred_element_type=jnp.float32)
    dec_proj = dec_proj.astype(jnp.bfloat16).reshape(SEQ, HEADS, 3, HEAD)
    queries = dec_proj[:, :, 0].astype(jnp.float32)
    keys = dec_proj[:, :, 1].astype(jnp.float32)
    values = dec_proj[:, :, 2].astype(jnp.float32)
    block = math.gcd(SEQ, 512)
    key_pos = jnp.arange(SEQ, dtype=jnp.int32)

    def one_block(index):
        begin = (index * block).astype(jnp.int32)
        query = lax.dynamic_slice_in_dim(queries, begin, block)
        query_pos = begin + jnp.arange(block, dtype=jnp.int32)
        scores = jnp.einsum('qhd,khd->hqk', query, keys) * HEAD ** (-0.5)
        scores = jnp.where(key_pos[None, None, :] <= query_pos[None, :, None], scores, -jnp.inf)
        weights = jnp.exp(scores - lax.optimization_barrier(jnp.max(scores, axis=-1, keepdims=True)))
        total = lax.optimization_barrier(jnp.sum(weights, axis=-1))
        mixed = jnp.einsum('hqk,khd->qhd', weights.astype(jnp.bfloat16).astype(jnp.float32), values)
        mixed = mixed / jnp.transpose(total, (1, 0))[..., None]
        return mixed.astype(jnp.bfloat16).reshape(block, D)
    dec_att = lax.map(one_block, jnp.arange(SEQ // block, dtype=jnp.int32)).reshape(SEQ, D)
    dec_branch = jnp.dot(dec_att, dec_out, preferred_element_type=jnp.float32)
    return (dec_in.astype(jnp.float32) + dec_branch).astype(jnp.bfloat16)
```

```python
import jax
import jax.numpy as jnp
from jax import lax
from jax.experimental import pallas as pl
from jax.experimental.pallas import tpu as pltpu
from jax.sharding import PartitionSpec as P

D = 1280
HEAD = 80
PATCH_SIDE = 16


eps_norm = 1e-06


def layer_norm(values, gain):
    center = values - jnp.mean(values, axis=-1, keepdims=True)
    spread = jnp.mean(center * center, axis=-1, keepdims=True)
    return center * lax.rsqrt(spread + eps_norm) * gain


def rms_norm(values, gain):
    return values * lax.rsqrt(jnp.mean(values * values, axis=-1, keepdims=True) + eps_norm) * gain


def add_rows(left, piece):
    return jnp.dot(left, piece, preferred_element_type=jnp.float32)


def image_attention(query, keys, values, keep):
    scores = jnp.einsum(
        "iqhd,ikhd->ihqk", query, keys, preferred_element_type=jnp.float32
    ) * HEAD ** (-0.5)
    scores = jnp.where(keep[:, None, None, :], scores, -jnp.inf)
    weights = jnp.exp(scores - jnp.max(scores, axis=-1, keepdims=True))
    total = jnp.sum(weights, axis=-1)
    mixed = jnp.einsum(
        "ihqk,ikhd->iqhd", weights.astype(jnp.bfloat16), values, preferred_element_type=jnp.float32
    )
    return (mixed / jnp.transpose(total, (0, 2, 1))[..., None]).astype(jnp.bfloat16)


def attend(state, query, query_pos, keys, values, key_pos):
    best, total, summed = state
    scores = jnp.einsum("qhd,khd->hqk", query, keys, preferred_element_type=jnp.float32) * HEAD ** (
        -0.5
    )
    allowed = key_pos[None, :] <= query_pos[:, None]
    scores = jnp.where(allowed[None], scores, -jnp.inf)
    new_best = jnp.maximum(best, jnp.max(scores, axis=-1))
    shift = jnp.where(jnp.isfinite(new_best), new_best, 0.0)
    weights = jnp.exp(scores - shift[..., None])
    fade = jnp.exp(best - shift)
    total = total * fade + jnp.sum(weights, axis=-1)
    update = jnp.einsum(
        "hqk,khd->hqd", weights.astype(jnp.bfloat16), values, preferred_element_type=jnp.float32
    )
    summed = summed * fade[..., None] + update
    return (new_best, total, summed)


def fresh_state(heads, count):
    return (
        jnp.full((heads, count), -jnp.inf, jnp.float32),
        jnp.zeros((heads, count), jnp.float32),
        jnp.zeros((heads, count, HEAD), jnp.float32),
    )


def finish(state):
    best, total, summed = state
    return summed / total[..., None]


def shards_any(
    patches,
    grid,
    vit_gain,
    vit_qkv,
    vit_out,
    merge_weight,
    text_embeds,
    prompt_pos,
    dec_gain,
    dec_qkv,
    dec_out,
):
    images, slots, part_width = patches.shape
    side = PATCH_SIDE
    half_side = side // 2
    rows_vit = images * slots
    local_heads = vit_qkv.shape[1] // (3 * HEAD)
    whole = lax.all_gather(patches, "narrow", axis=2, tiled=True)
    normed = (
        layer_norm(whole.astype(jnp.float32), vit_gain).astype(jnp.bfloat16).reshape(rows_vit, D)
    )
    projected = add_rows(normed, lax.all_gather(vit_qkv, "wide", axis=0, tiled=True))
    projected = projected.astype(jnp.bfloat16).reshape(images, slots, local_heads, 3, HEAD)
    slot_ids = jnp.arange(slots, dtype=jnp.int32)
    keep = ((slot_ids // side)[None, :] < grid[:, 0:1]) & (
        (slot_ids % side)[None, :] < grid[:, 1:2]
    )
    attended = image_attention(
        projected[:, :, :, 0], projected[:, :, :, 1], projected[:, :, :, 2], keep
    )
    attended = attended.reshape(rows_vit, local_heads * HEAD)
    vit_partial = jnp.dot(
        attended,
        lax.all_gather(vit_out, "wide", axis=1, tiled=True),
        preferred_element_type=jnp.float32,
    )
    vit_branch = lax.psum_scatter(vit_partial, "narrow", scatter_dimension=1, tiled=True)
    after = (patches.reshape(rows_vit, part_width).astype(jnp.float32) + vit_branch).astype(
        jnp.bfloat16
    )
    grouped = after.reshape(images, half_side, 2, half_side, 2, part_width).transpose(
        0, 1, 3, 2, 4, 5
    )
    grouped = grouped.reshape(images * half_side * half_side, 4 * part_width)
    piece = lax.all_gather(merge_weight, "wide", axis=2, tiled=True)
    flat_piece = piece.reshape(4 * part_width, piece.shape[2])
    merge_partial = jnp.dot(grouped, flat_piece, preferred_element_type=jnp.float32)
    merged = lax.psum_scatter(merge_partial, "narrow", scatter_dimension=1, tiled=True).astype(
        jnp.bfloat16
    )
    text_rows = text_embeds.shape[0]
    half_rows = text_rows // 2
    wide_index = lax.axis_index("wide")
    offsets = jnp.arange(text_rows, dtype=jnp.int32)
    mine = wide_index * text_rows + offsets
    flat_pos = prompt_pos.reshape(-1)
    select = (mine[:, None] == flat_pos[None, :]).astype(jnp.bfloat16)
    routed = jnp.dot(
        select,
        lax.all_gather(merged, "wide", axis=0, tiled=True),
        preferred_element_type=jnp.float32,
    )
    is_image = jnp.any(mine[:, None] == flat_pos[None, :], axis=1)
    dec_in = jnp.where(is_image[:, None], routed.astype(jnp.bfloat16), text_embeds)
    dec_whole = lax.all_gather(dec_in, "narrow", axis=1, tiled=True)
    dec_normed = rms_norm(dec_whole.astype(jnp.float32), dec_gain).astype(jnp.bfloat16)
    dec_proj = add_rows(dec_normed, lax.all_gather(dec_qkv, "wide", axis=0, tiled=True))
    dec_proj = dec_proj.astype(jnp.bfloat16).reshape(text_rows, local_heads, 3, HEAD)
    queries = dec_proj[:, :, 0]
    keys = dec_proj[:, :, 1].reshape(text_rows, local_heads * HEAD)
    values = dec_proj[:, :, 2].reshape(text_rows, local_heads * HEAD)
    low_pos = mine[:half_rows]
    high_pos = mine[half_rows:]
    low_query = queries[:half_rows]
    high_query = queries[half_rows:]
    start_state = (
        fresh_state(local_heads, half_rows),
        fresh_state(local_heads, text_rows - half_rows),
    )
    key_piece = lax.all_gather(keys, "wide", axis=0, tiled=True)
    value_piece = lax.all_gather(values, "wide", axis=0, tiled=True)
    count = key_piece.shape[0]
    span_rows = count
    while span_rows > 2048 and span_rows % 2 == 0:
        span_rows = span_rows // 2
    key_heads = key_piece.reshape(count, local_heads, HEAD)
    value_heads = value_piece.reshape(count, local_heads, HEAD)

    def one_span(index, carry):
        begin = (index * span_rows).astype(jnp.int32)
        key_span = lax.dynamic_slice_in_dim(key_heads, begin, span_rows)
        value_span = lax.dynamic_slice_in_dim(value_heads, begin, span_rows)
        key_pos = begin + jnp.arange(span_rows, dtype=jnp.int32)
        earliest = jnp.min(key_pos)
        first = lax.cond(
            earliest <= jnp.max(low_pos),
            lambda inner: attend(inner, low_query, low_pos, key_span, value_span, key_pos),
            lambda inner: inner,
            carry[0],
        )
        second = lax.cond(
            earliest <= jnp.max(high_pos),
            lambda inner: attend(inner, high_query, high_pos, key_span, value_span, key_pos),
            lambda inner: inner,
            carry[1],
        )
        return (first, second)

    final = lax.fori_loop(0, count // span_rows, one_span, start_state)
    heads_out = jnp.concatenate([finish(final[0]), finish(final[1])], axis=1)
    heads_out = (
        heads_out.transpose(1, 0, 2).reshape(text_rows, local_heads * HEAD).astype(jnp.bfloat16)
    )
    dec_partial = jnp.dot(
        heads_out,
        lax.all_gather(dec_out, "wide", axis=1, tiled=True),
        preferred_element_type=jnp.float32,
    )
    dec_branch = lax.psum_scatter(
        dec_partial.astype(jnp.bfloat16), "narrow", scatter_dimension=1, tiled=True
    ).astype(jnp.float32)
    result = (dec_in.astype(jnp.float32) + dec_branch).astype(jnp.bfloat16)
    return result


CROSS_X = [(w, w ^ 2) for w in range(16)]
CROSS_C = [(w, w ^ 1) for w in range(16)]
CROSS_Y = [(0, 1), (1, 0)]
GROUPS_Z = [[b, 4 + b, 8 + b, 12 + b] for b in range(4)]
GROUPS_B = [[4 * z + b for b in range(4)] for z in range(4)]
FOUR = ((0, 0), (0, 1), (1, 0), (1, 1))
VMEM = pl.BlockSpec(memory_space=pltpu.VMEM)
SMEM = pl.BlockSpec(memory_space=pltpu.SMEM)
F32 = jnp.float32
BF16 = jnp.bfloat16
GRANT = 48 * 1024 * 1024


def over_x(value):
    return lax.ppermute(value, "wide", CROSS_X)


def over_c(value):
    return lax.ppermute(value, "wide", CROSS_C)


def over_y(value):
    return lax.ppermute(value, "narrow", CROSS_Y)


def share_xy(value):
    half = value.shape[0] // 2
    from_x = over_x(value)
    from_y = over_y(value)
    corner = [over_y(from_x[:half]), over_x(from_y[half:])]
    return [[[value], [from_y]], [[from_x], corner]]


def share_xyc(value):
    pieces = share_xy(value)
    found = {}
    for ex in (0, 1):
        for ec in (0, 1):
            found[(ex, ec)] = [
                [over_c(part) if ec else part for part in pieces[ex][ey]] for ey in (0, 1)
            ]
    return found


def flat_parts(pieces):
    return [part for key in FOUR for ey in (0, 1) for part in pieces[key][ey]]


def read_parts(refs):
    found, at = {}, 0
    for key in FOUR:
        found[key] = []
        for ey in (0, 1):
            many = 2 if (key[0] and ey) else 1
            found[key].append(refs[at : at + many])
            at += many
    return found


def whole_of(refs):
    if len(refs) == 1:
        return refs[0][...]
    return jnp.concatenate([ref[...] for ref in refs], axis=0)


def contract(left, right, left_dim, right_dim):
    return lax.dot_general(
        left, right, (((left_dim,), (right_dim,)), ((), ())), preferred_element_type=F32
    )


def encode_kernel(*refs):
    parts = read_parts(refs[:10])
    gain, weight, keep, out = refs[10:]
    for slot, key in enumerate(FOUR):
        own = whole_of(parts[key][0]).astype(F32)
        other = whole_of(parts[key][1]).astype(F32)
        mean = (
            jnp.sum(own, axis=-1, keepdims=True) + jnp.sum(other, axis=-1, keepdims=True)
        ) * (1.0 / D)
        own = own - mean
        other = other - mean
        spread = (
            jnp.sum(own * own, axis=-1, keepdims=True)
            + jnp.sum(other * other, axis=-1, keepdims=True)
        ) * (1.0 / D)
        scale = lax.rsqrt(spread + eps_norm)
        own = (own * scale * gain[:, : D // 2]).astype(BF16)
        other = (other * scale * gain[:, D // 2 :]).astype(BF16)
        proj = contract(own, weight[: D // 2, :], 1, 0) + contract(
            other, weight[D // 2 :, :], 1, 0
        )
        proj = proj.astype(BF16)
        live = keep[:, slot : slot + 1] > 0.0
        for head in (0, 1):
            base = head * 3 * HEAD
            query = proj[:, base : base + HEAD]
            key_rows = proj[:, base + HEAD : base + 2 * HEAD]
            value_rows = proj[:, base + 2 * HEAD : base + 3 * HEAD]
            scores = contract(key_rows, query, 1, 1) * HEAD ** (-0.5)
            scores = jnp.where(live, scores, -jnp.inf)
            weights = jnp.exp(scores - jnp.max(scores, axis=0, keepdims=True))
            total = jnp.sum(weights, axis=0, keepdims=True)
            mixed = contract(value_rows, weights.astype(BF16), 0, 0)
            out[head * HEAD : (head + 1) * HEAD, slot * 256 : (slot + 1) * 256] = (
                mixed / total
            ).astype(BF16)


def merge_kernel(where, *refs):
    parts = read_parts(refs[:10])
    residual = refs[10:14]
    out_weight, weight, keep_out, send_out, heads, grouped, summed = refs[14:]
    here = where[1] * 2 + where[2]
    for code, key in enumerate(FOUR):
        for ey in (0, 1):
            base = ey * (D // 2) + 2 * HEAD * jnp.bitwise_xor(here, code)
            rows = 0
            for ref in parts[key][ey]:
                count = ref.shape[0]
                at = pl.ds(pl.multiple_of(base + rows, 16), count)
                for slot in range(4):
                    other = slot ^ code
                    heads[at, slot * 256 : (slot + 1) * 256] = ref[
                        :, other * 256 : (other + 1) * 256
                    ]
                rows += count
    row = lax.broadcasted_iota(jnp.int32, (256, 256), 0)
    column = lax.broadcasted_iota(jnp.int32, (256, 256), 1)
    sub, token = row // 64, row % 64
    source = (2 * (token // 8) + sub // 2) * 16 + 2 * (token % 8) + sub % 2
    order = jnp.where(column == source, 1.0, 0.0).astype(BF16)
    for slot in range(4):
        branch = contract(heads[:, slot * 256 : (slot + 1) * 256], out_weight[...], 0, 0)
        after = (residual[slot][...].astype(F32) + branch).astype(BF16)
        sorted_rows = contract(order, after, 1, 0).astype(BF16)
        for sub_patch in range(4):
            grouped[sub_patch, slot * 64 : (slot + 1) * 64, :] = sorted_rows[
                sub_patch * 64 : (sub_patch + 1) * 64
            ]
    total = contract(grouped[0], weight[0], 1, 1)
    for sub_patch in range(1, 4):
        total = total + contract(grouped[sub_patch], weight[sub_patch], 1, 1)
    summed[...] = total
    mine = where[3] * 128
    keep_out[...] = summed[pl.ds(pl.multiple_of(mine, 128), 128), :]
    send_out[...] = summed[pl.ds(pl.multiple_of(128 - mine, 128), 128), :]


def place_kernel(where, *refs):
    parts = read_parts(refs[:10])
    gain, weight, flat_pos, text_proj, query, key_out, value_out, routed, proj = refs[10:]
    tokens = {}
    for sx in (0, 1):
        blocks = []
        for ex, ec in FOUR:
            rows = whole_of(parts[(ex, ec)][sx ^ ex])
            if ec:
                rows = jnp.concatenate(
                    [rows[64 * (at ^ 1) : 64 * (at ^ 1) + 64] for at in range(8)], axis=0
                )
            blocks.append(rows)
        tokens[sx] = blocks
        wide = [block.astype(F32) for block in blocks]
        squares = sum(jnp.sum(block * block, axis=-1, keepdims=True) for block in wide)
        scale = lax.rsqrt(squares * (1.0 / D) + eps_norm)
        total = 0.0
        for at, block in enumerate(wide):
            normed = (block * scale * gain[at : at + 1, :]).astype(BF16)
            total = total + contract(normed, weight[at], 1, 0)
        proj[sx * 512 : (sx + 1) * 512, :] = total.astype(BF16)
    positions = flat_pos[...]
    columns = positions.shape[1]
    block_rows = query.shape[0] // 8
    for block in range(8):
        first = (2 * block + where[2]) * block_rows
        row = first + lax.broadcasted_iota(jnp.int32, (block_rows, columns), 0)
        hit = row == positions
        select = jnp.where(hit, 1.0, 0.0)
        image = jnp.max(select, axis=-1, keepdims=True) > 0.0
        moved = contract(select.astype(BF16), proj[...], 1, 0)
        at = slice(block * block_rows, (block + 1) * block_rows)
        rows = jnp.where(image, moved, text_proj[at, :].astype(F32)).astype(BF16)
        query[at, :] = rows[:, :128]
        key_out[at, :] = rows[:, 128:256]
        value_out[at, :] = rows[:, 256:]
    own_block = 4 * where[0] + 2 * where[1] + where[2]
    row = own_block * block_rows + lax.broadcasted_iota(jnp.int32, (block_rows, columns), 0)
    select = jnp.where(row == positions, 1.0, 0.0).astype(BF16)
    for at in range(4):
        moved = contract(select[:, :512], tokens[0][at], 1, 0) + contract(
            select[:, 512:], tokens[1][at], 1, 0
        )
        routed[at] = moved.astype(BF16)


def decode_kernel(where, query, own_key, own_value, other_key, other_value, out):
    rows = query.shape[0] // 8
    later = where[2] > 0
    for block in range(8):
        count = (block + 1) * rows
        asked = query[block * rows : count, :]
        own = contract(asked, own_key[:count, :], 1, 1) * HEAD ** (-0.5)
        other = contract(asked, other_key[:count, :], 1, 1) * HEAD ** (-0.5)
        row = lax.broadcasted_iota(jnp.int32, (rows, count), 0) + block * rows
        column = lax.broadcasted_iota(jnp.int32, (rows, count), 1)
        own = jnp.where(column <= row, own, -jnp.inf)
        limit = jnp.where(later, count, block * rows)
        other = jnp.where(column < limit, other, -jnp.inf)
        best = jnp.maximum(
            jnp.max(own, axis=-1, keepdims=True), jnp.max(other, axis=-1, keepdims=True)
        )
        own = jnp.exp(own - best)
        other = jnp.exp(other - best)
        total = jnp.sum(own, axis=-1, keepdims=True) + jnp.sum(other, axis=-1, keepdims=True)
        mixed = contract(own.astype(BF16), own_value[:count, :], 1, 0) + contract(
            other.astype(BF16), other_value[:count, :], 1, 0
        )
        mixed = (mixed / total).astype(BF16)
        out[2 * block] = mixed
        out[2 * block + 1] = mixed


def finish_kernel(where, heads, weight, residual, out):
    total = residual[...].astype(F32)
    branch = 0.0
    for at in range(16):
        chip, y = at // 2, at % 2
        base = jnp.bitwise_xor(where[3], y) * (D // 2) + chip * HEAD
        rows = weight[pl.ds(pl.multiple_of(base, 16), HEAD), :]
        branch = branch + contract(heads[at][:, :HEAD], rows, 1, 0)
    out[...] = (total + branch).astype(BF16)


def run(kernel, shapes, scratch, *operands, scalars=None):
    specs = ([SMEM] if scalars is not None else []) + [VMEM] * len(operands)
    given = ([scalars] if scalars is not None else []) + list(operands)
    single = not isinstance(shapes, (list, tuple))
    return pl.pallas_call(
        kernel,
        out_shape=shapes,
        in_specs=specs,
        out_specs=VMEM if single else [VMEM] * len(shapes),
        scratch_shapes=scratch,
        compiler_params=pltpu.CompilerParams(vmem_limit_bytes=GRANT),
    )(*given)


def share_out(block, z, y, w):
    turned = block.T
    send = [(2 * w_ + 1 - w_ // 8, 2 * w_ + w_ // 8) for w_ in range(16)]
    both = jnp.stack([turned, lax.ppermute(turned, ("wide", "narrow"), send)])
    far = [(2 * w_ + w_ // 8, 2 * (w_ ^ 8) + w_ // 8) for w_ in range(16)]
    moved = lax.ppermute(both, ("wide", "narrow"), far)
    held = jnp.where(z // 2 == y, both, moved)[None]
    near = [(w_, w_ ^ 4) for w_ in range(16)]
    held = jnp.concatenate([held, lax.ppermute(held, "wide", near)])
    held = jnp.concatenate([held, over_x(held)])
    held = jnp.concatenate([held, over_c(held)])
    rows = []
    for at in range(8):
        flip = at ^ (w % 8)
        index = 4 * (flip % 2) + 2 * ((flip // 2) % 2) + flip // 4
        rows.append(lax.dynamic_index_in_dim(held, index, 0, keepdims=False))
    whole = jnp.stack(rows)
    return whole.transpose(1, 3, 0, 2).reshape(2 * block.shape[0], 8 * block.shape[1])


def shards_fast(
    patches,
    grid,
    vit_gain,
    vit_qkv,
    vit_out,
    merge_weight,
    text_embeds,
    prompt_pos,
    dec_gain,
    dec_qkv,
    dec_out,
):
    w = lax.axis_index("wide").astype(jnp.int32)
    y = lax.axis_index("narrow").astype(jnp.int32)
    z, x, c = w // 4, (w // 2) % 2, w % 2
    where = jnp.stack([z, x, c, y])
    half = D // 2
    text_rows = text_embeds.shape[0]

    def own_first(value):
        return jnp.roll(value, -half * y, axis=0)

    patch_parts = share_xyc(patches[0])
    columns = vit_qkv.shape[1] // 4
    sliced = vit_qkv.reshape(-1, 4, columns).transpose(1, 0, 2)
    sliced = lax.all_to_all(sliced, "wide", 0, 0, axis_index_groups=GROUPS_B, tiled=True)
    sliced = sliced.reshape(-1, columns)
    vit_weight = lax.all_gather(sliced, "wide", axis_index_groups=GROUPS_Z, axis=0, tiled=True)
    merge_turned = merge_weight.transpose(0, 2, 1)
    merge_rows = lax.all_gather(
        merge_turned, "wide", axis_index_groups=GROUPS_Z, axis=1, tiled=True
    )
    vit_out_rows = share_out(vit_out, z, y, w)
    codes = jnp.arange(4, dtype=jnp.int32)
    live = prompt_pos[4 * z + jnp.bitwise_xor(2 * x + c, codes)] >= 0
    side = PATCH_SIDE // 2
    live = jnp.repeat(jnp.repeat(live.reshape(4, side, side), 2, axis=1), 2, axis=2)
    live = live.reshape(4, 4 * side * side).T.astype(F32)
    attended = run(
        encode_kernel,
        jax.ShapeDtypeStruct((2 * HEAD, 4 * patches.shape[1]), BF16),
        [],
        *flat_parts(patch_parts),
        own_first(vit_gain)[None],
        own_first(vit_weight),
        live,
    )
    head_parts = share_xyc(attended)
    part = jax.ShapeDtypeStruct((128, 320), F32)
    kept, sent = run(
        merge_kernel,
        [part, part],
        [
            pltpu.VMEM((D, 4 * patches.shape[1]), BF16),
            pltpu.VMEM((4, 256, half), BF16),
            pltpu.VMEM((256, 320), F32),
        ],
        *flat_parts(head_parts),
        *[patch_parts[key][0][0] for key in FOUR],
        vit_out_rows,
        merge_rows,
        scalars=where,
    )
    merged = (kept + over_y(sent)).astype(BF16)
    around = [merged] + [
        lax.ppermute(merged, "wide", [(w_, (w_ + 4 * k) % 16) for w_ in range(16)])
        for k in (1, 2, 3)
    ]
    token_parts = share_xyc(jnp.concatenate(around))

    third = dec_qkv.shape[1] // 16
    pieces = dec_qkv.reshape(-1, 16, third).transpose(1, 0, 2)
    pieces = lax.all_to_all(pieces, "wide", 0, 0, tiled=True).reshape(-1, third)
    partner = over_c(pieces)
    head_weight = jnp.where(
        c == 0,
        jnp.concatenate([pieces, partner], axis=1),
        jnp.concatenate([partner, pieces], axis=1),
    )
    head_weight = jnp.pad(head_weight.reshape(D, 3, HEAD), ((0, 0), (0, 0), (0, 128 - HEAD)))
    head_weight = head_weight.reshape(D, 384)

    def by_partner(value):
        split = value.reshape((4, 4, D // 16) + value.shape[1:])
        taken = [
            lax.dynamic_index_in_dim(split, jnp.bitwise_xor(2 * x + c, code), 1, keepdims=False)
            for code in range(4)
        ]
        return jnp.stack(taken).reshape((4, D // 4) + value.shape[1:])

    stacked = lax.all_gather(text_embeds, "wide", axis_index_groups=GROUPS_Z, axis=0, tiled=True)
    text_parts = share_xy(stacked)
    text_gain = own_first(dec_gain)
    text_weight = own_first(head_weight)
    text_proj = []
    for ex in (0, 1):
        rows = jnp.concatenate([jnp.concatenate(p, axis=0) for p in text_parts[ex]], axis=1)
        normed = rms_norm(rows.astype(F32), text_gain).astype(BF16)
        text_proj.append(add_rows(normed, text_weight).astype(BF16).reshape(4, text_rows, 384))
    first = jnp.where(x == 0, text_proj[0], text_proj[1])
    second = jnp.where(x == 0, text_proj[1], text_proj[0])
    text_proj = jnp.stack([first, second], axis=1).reshape(8 * text_rows, 384)

    sx = jnp.arange(2, dtype=jnp.int32)[:, None, None]
    k = jnp.arange(4, dtype=jnp.int32)[None, :, None]
    sc = jnp.arange(2, dtype=jnp.int32)[None, None, :]
    image = 4 * ((z - k) % 4) + 2 * (sx ^ x ^ y) + (sc ^ c)
    flat_pos = prompt_pos[image.reshape(-1)].reshape(1, -1)
    lanes = jax.ShapeDtypeStruct((8 * text_rows, 128), BF16)
    query, key, value, routed = run(
        place_kernel,
        [lanes, lanes, lanes, jax.ShapeDtypeStruct((4, text_rows, 320), BF16)],
        [pltpu.VMEM((1024, 384), BF16)],
        *flat_parts(token_parts),
        by_partner(dec_gain),
        by_partner(head_weight),
        flat_pos,
        text_proj,
        scalars=where,
    )
    heads = run(
        decode_kernel,
        jax.ShapeDtypeStruct((16, text_rows, 128), BF16),
        [],
        query,
        key,
        value,
        over_c(key),
        over_c(value),
        scalars=where,
    )
    by_core = [[2 * w_ + y_ for w_ in range(c_, 16, 2) for y_ in (0, 1)] for c_ in (0, 1)]
    heads = lax.all_to_all(
        heads, ("wide", "narrow"), 0, 0, axis_index_groups=by_core, tiled=True
    )
    dec_out_rows = share_out(dec_out, z, y, w)
    routed = routed.reshape(4, text_rows, 4, D // 16)
    routed = lax.dynamic_slice_in_dim(routed, 2 * y, 2, axis=2)
    ordered = jnp.stack(
        [
            lax.dynamic_index_in_dim(routed, jnp.bitwise_xor(2 * x + c, code), 0, keepdims=False)
            for code in range(4)
        ]
    )
    ordered = ordered.transpose(1, 2, 0, 3).reshape(text_rows, half)
    mine = w * text_rows + jnp.arange(text_rows, dtype=jnp.int32)
    is_image = jnp.any(mine[:, None] == prompt_pos.reshape(1, -1), axis=1)
    dec_in = jnp.where(is_image[:, None], ordered, text_embeds)
    return run(
        finish_kernel,
        jax.ShapeDtypeStruct(text_embeds.shape, BF16),
        [],
        heads,
        dec_out_rows,
        dec_in,
        scalars=where,
    )


def solution(mesh):
    placed = (
        P("wide", None, "narrow"),
        P("wide", None),
        P(),
        P("wide", "narrow"),
        P("narrow", "wide"),
        P(None, "narrow", "wide"),
        P("wide", "narrow"),
        P(),
        P(),
        P("wide", "narrow"),
        P("narrow", "wide"),
    )
    sizes = (mesh.shape["wide"], mesh.shape["narrow"])
    shards = shards_fast if sizes == (16, 2) else shards_any
    return jax.shard_map(
        shards, mesh=mesh, in_specs=placed, out_specs=P("wide", "narrow"), check_vma=False
    )
```

```python
import jax
import jax.numpy as jnp
from jax import lax
from jax.experimental import pallas as pl
from jax.experimental.pallas import tpu as pltpu
from jax.sharding import PartitionSpec as P

D = 1280
HEAD = 80
PATCH_SIDE = 16


eps_norm = 1e-06


def layer_norm(values, gain):
    center = values - jnp.mean(values, axis=-1, keepdims=True)
    spread = jnp.mean(center * center, axis=-1, keepdims=True)
    return center * lax.rsqrt(spread + eps_norm) * gain


def rms_norm(values, gain):
    return values * lax.rsqrt(jnp.mean(values * values, axis=-1, keepdims=True) + eps_norm) * gain


def add_rows(left, piece):
    return jnp.dot(left, piece, preferred_element_type=jnp.float32)


def image_attention(query, keys, values, keep):
    scores = jnp.einsum(
        "iqhd,ikhd->ihqk", query, keys, preferred_element_type=jnp.float32
    ) * HEAD ** (-0.5)
    scores = jnp.where(keep[:, None, None, :], scores, -jnp.inf)
    weights = jnp.exp(scores - jnp.max(scores, axis=-1, keepdims=True))
    total = jnp.sum(weights, axis=-1)
    mixed = jnp.einsum(
        "ihqk,ikhd->iqhd", weights.astype(jnp.bfloat16), values, preferred_element_type=jnp.float32
    )
    return (mixed / jnp.transpose(total, (0, 2, 1))[..., None]).astype(jnp.bfloat16)


def attend(state, query, query_pos, keys, values, key_pos):
    best, total, summed = state
    scores = jnp.einsum("qhd,khd->hqk", query, keys, preferred_element_type=jnp.float32) * HEAD ** (
        -0.5
    )
    allowed = key_pos[None, :] <= query_pos[:, None]
    scores = jnp.where(allowed[None], scores, -jnp.inf)
    new_best = jnp.maximum(best, jnp.max(scores, axis=-1))
    shift = jnp.where(jnp.isfinite(new_best), new_best, 0.0)
    weights = jnp.exp(scores - shift[..., None])
    fade = jnp.exp(best - shift)
    total = total * fade + jnp.sum(weights, axis=-1)
    update = jnp.einsum(
        "hqk,khd->hqd", weights.astype(jnp.bfloat16), values, preferred_element_type=jnp.float32
    )
    summed = summed * fade[..., None] + update
    return (new_best, total, summed)


def fresh_state(heads, count):
    return (
        jnp.full((heads, count), -jnp.inf, jnp.float32),
        jnp.zeros((heads, count), jnp.float32),
        jnp.zeros((heads, count, HEAD), jnp.float32),
    )


def finish(state):
    best, total, summed = state
    return summed / total[..., None]


def shards_any(
    patches,
    grid,
    vit_gain,
    vit_qkv,
    vit_out,
    merge_weight,
    text_embeds,
    prompt_pos,
    dec_gain,
    dec_qkv,
    dec_out,
):
    images, slots, part_width = patches.shape
    side = PATCH_SIDE
    half_side = side // 2
    rows_vit = images * slots
    local_heads = vit_qkv.shape[1] // (3 * HEAD)
    whole = lax.all_gather(patches, "narrow", axis=2, tiled=True)
    normed = (
        layer_norm(whole.astype(jnp.float32), vit_gain).astype(jnp.bfloat16).reshape(rows_vit, D)
    )
    projected = add_rows(normed, lax.all_gather(vit_qkv, "wide", axis=0, tiled=True))
    projected = projected.astype(jnp.bfloat16).reshape(images, slots, local_heads, 3, HEAD)
    slot_ids = jnp.arange(slots, dtype=jnp.int32)
    keep = ((slot_ids // side)[None, :] < grid[:, 0:1]) & (
        (slot_ids % side)[None, :] < grid[:, 1:2]
    )
    attended = image_attention(
        projected[:, :, :, 0], projected[:, :, :, 1], projected[:, :, :, 2], keep
    )
    attended = attended.reshape(rows_vit, local_heads * HEAD)
    vit_partial = jnp.dot(
        attended,
        lax.all_gather(vit_out, "wide", axis=1, tiled=True),
        preferred_element_type=jnp.float32,
    )
    vit_branch = lax.psum_scatter(vit_partial, "narrow", scatter_dimension=1, tiled=True)
    after = (patches.reshape(rows_vit, part_width).astype(jnp.float32) + vit_branch).astype(
        jnp.bfloat16
    )
    grouped = after.reshape(images, half_side, 2, half_side, 2, part_width).transpose(
        0, 1, 3, 2, 4, 5
    )
    grouped = grouped.reshape(images * half_side * half_side, 4 * part_width)
    piece = lax.all_gather(merge_weight, "wide", axis=2, tiled=True)
    flat_piece = piece.reshape(4 * part_width, piece.shape[2])
    merge_partial = jnp.dot(grouped, flat_piece, preferred_element_type=jnp.float32)
    merged = lax.psum_scatter(merge_partial, "narrow", scatter_dimension=1, tiled=True).astype(
        jnp.bfloat16
    )
    text_rows = text_embeds.shape[0]
    half_rows = text_rows // 2
    wide_index = lax.axis_index("wide")
    offsets = jnp.arange(text_rows, dtype=jnp.int32)
    mine = wide_index * text_rows + offsets
    flat_pos = prompt_pos.reshape(-1)
    select = (mine[:, None] == flat_pos[None, :]).astype(jnp.bfloat16)
    routed = jnp.dot(
        select,
        lax.all_gather(merged, "wide", axis=0, tiled=True),
        preferred_element_type=jnp.float32,
    )
    is_image = jnp.any(mine[:, None] == flat_pos[None, :], axis=1)
    dec_in = jnp.where(is_image[:, None], routed.astype(jnp.bfloat16), text_embeds)
    dec_whole = lax.all_gather(dec_in, "narrow", axis=1, tiled=True)
    dec_normed = rms_norm(dec_whole.astype(jnp.float32), dec_gain).astype(jnp.bfloat16)
    dec_proj = add_rows(dec_normed, lax.all_gather(dec_qkv, "wide", axis=0, tiled=True))
    dec_proj = dec_proj.astype(jnp.bfloat16).reshape(text_rows, local_heads, 3, HEAD)
    queries = dec_proj[:, :, 0]
    keys = dec_proj[:, :, 1].reshape(text_rows, local_heads * HEAD)
    values = dec_proj[:, :, 2].reshape(text_rows, local_heads * HEAD)
    low_pos = mine[:half_rows]
    high_pos = mine[half_rows:]
    low_query = queries[:half_rows]
    high_query = queries[half_rows:]
    start_state = (
        fresh_state(local_heads, half_rows),
        fresh_state(local_heads, text_rows - half_rows),
    )
    key_piece = lax.all_gather(keys, "wide", axis=0, tiled=True)
    value_piece = lax.all_gather(values, "wide", axis=0, tiled=True)
    count = key_piece.shape[0]
    span_rows = count
    while span_rows > 2048 and span_rows % 2 == 0:
        span_rows = span_rows // 2
    key_heads = key_piece.reshape(count, local_heads, HEAD)
    value_heads = value_piece.reshape(count, local_heads, HEAD)

    def one_span(index, carry):
        begin = (index * span_rows).astype(jnp.int32)
        key_span = lax.dynamic_slice_in_dim(key_heads, begin, span_rows)
        value_span = lax.dynamic_slice_in_dim(value_heads, begin, span_rows)
        key_pos = begin + jnp.arange(span_rows, dtype=jnp.int32)
        earliest = jnp.min(key_pos)
        first = lax.cond(
            earliest <= jnp.max(low_pos),
            lambda inner: attend(inner, low_query, low_pos, key_span, value_span, key_pos),
            lambda inner: inner,
            carry[0],
        )
        second = lax.cond(
            earliest <= jnp.max(high_pos),
            lambda inner: attend(inner, high_query, high_pos, key_span, value_span, key_pos),
            lambda inner: inner,
            carry[1],
        )
        return (first, second)

    final = lax.fori_loop(0, count // span_rows, one_span, start_state)
    heads_out = jnp.concatenate([finish(final[0]), finish(final[1])], axis=1)
    heads_out = (
        heads_out.transpose(1, 0, 2).reshape(text_rows, local_heads * HEAD).astype(jnp.bfloat16)
    )
    dec_partial = jnp.dot(
        heads_out,
        lax.all_gather(dec_out, "wide", axis=1, tiled=True),
        preferred_element_type=jnp.float32,
    )
    dec_branch = lax.psum_scatter(
        dec_partial.astype(jnp.bfloat16), "narrow", scatter_dimension=1, tiled=True
    ).astype(jnp.float32)
    result = (dec_in.astype(jnp.float32) + dec_branch).astype(jnp.bfloat16)
    return result


CROSS_X = [(w, w ^ 2) for w in range(16)]
CROSS_C = [(w, w ^ 1) for w in range(16)]
CROSS_Y = [(0, 1), (1, 0)]
GROUPS_Z = [[b, 4 + b, 8 + b, 12 + b] for b in range(4)]
GROUPS_B = [[4 * z + b for b in range(4)] for z in range(4)]
FOUR = ((0, 0), (0, 1), (1, 0), (1, 1))
SMEM = pl.BlockSpec(memory_space=pltpu.SMEM)
F32 = jnp.float32
BF16 = jnp.bfloat16
GRANT = 48 * 1024 * 1024
MOST = 59 * 1024 * 1024


def over_x(value):
    return lax.ppermute(value, "wide", CROSS_X)


def over_c(value):
    return lax.ppermute(value, "wide", CROSS_C)


def over_y(value):
    return lax.ppermute(value, "narrow", CROSS_Y)


RING_Z = [(4 * a + b, 4 * n + b) for a, n in ((0, 1), (1, 3), (3, 2), (2, 0)) for b in range(4)]


def next_z(value):
    return lax.ppermute(value, "wide", RING_Z)


def z_behind(z, steps):
    place = lax.rem(jnp.bitwise_xor(z, z // 2) + 4 - steps, 4)
    return jnp.bitwise_xor(place, place // 2)


def around_z(value):
    return [value] + [
        lax.ppermute(value, "wide", [(w, (w + 4 * k) % 16) for w in range(16)]) for k in (1, 2, 3)
    ]


def over_xy(value):
    both = [(2 * w + y, 2 * (w ^ 2) + 1 - y) for w in range(16) for y in (0, 1)]
    return lax.ppermute(value, ("wide", "narrow"), both)


def share_xy(value):
    return [[value, over_y(value)], [over_x(value), over_xy(value)]]


def share_xyc(value):
    pieces = share_xy(value)
    return [
        over_c(pieces[ex][ey]) if ec else pieces[ex][ey]
        for ex, ec in FOUR
        for ey in (0, 1)
    ]


def contract(left, right, left_dim, right_dim):
    return lax.dot_general(
        left, right, (((left_dim,), (right_dim,)), ((), ())), preferred_element_type=F32
    )


def patch_order():
    row = lax.broadcasted_iota(jnp.int32, (256, 256), 0)
    column = lax.broadcasted_iota(jnp.int32, (256, 256), 1)
    sub, token = row // 64, row % 64
    source = (2 * (token // 8) + sub // 2) * 16 + 2 * (token % 8) + sub % 2
    return jnp.where(column == source, 1.0, 0.0).astype(BF16)


def norm_kernel(where, *refs):
    parts = refs[:8]
    gain, normed, residual = refs[8:]
    order = patch_order()
    own_gain = gain[pl.ds(where[3], 1), :]
    other_gain = gain[pl.ds(1 - where[3], 1), :]
    for slot in range(4):
        raw = parts[2 * slot][...]
        own = raw.astype(F32)
        other = parts[2 * slot + 1][...].astype(F32)
        mean = (
            jnp.sum(own, axis=-1, keepdims=True) + jnp.sum(other, axis=-1, keepdims=True)
        ) * (1.0 / D)
        own = own - mean
        other = other - mean
        spread = (
            jnp.sum(own * own, axis=-1, keepdims=True)
            + jnp.sum(other * other, axis=-1, keepdims=True)
        ) * (1.0 / D)
        scale = lax.rsqrt(spread + eps_norm)
        own = (own * scale * own_gain).astype(BF16)
        other = (other * scale * other_gain).astype(BF16)
        at = slice(slot * 256, (slot + 1) * 256)
        normed[at, : D // 2] = contract(order, own, 1, 0).astype(BF16)
        normed[at, D // 2 :] = contract(order, other, 1, 0).astype(BF16)
        residual[:, at] = contract(raw, order, 0, 1).astype(BF16)


def own_half_first(where, block):
    row = block * (D // 16) - where[3] * (D // 2)
    return pl.multiple_of(jnp.where(row < 0, row + D, row), 16)


def encode_kernel(where, normed, first, second, third, fourth, keep, out, weight):
    block = D // 16
    here = where[1] * 2 + where[2]
    for steps, piece in enumerate((first, second, third, fourth)):
        z = z_behind(where[0], steps)
        for code in range(4):
            row = own_half_first(where, 4 * z + jnp.bitwise_xor(here, code))
            weight[pl.ds(row, block), :] = piece[code * block : (code + 1) * block, :]
    for slot in range(4):
        proj = contract(normed[slot * 256 : (slot + 1) * 256, :], weight[...], 1, 0).astype(BF16)
        live = keep[:, slot : slot + 1] > 0.0
        for head in (0, 1):
            base = head * 3 * HEAD
            query = proj[:, base : base + HEAD]
            key_rows = proj[:, base + HEAD : base + 2 * HEAD]
            value_rows = proj[:, base + 2 * HEAD : base + 3 * HEAD]
            scores = contract(key_rows, query, 1, 1) * HEAD ** (-0.5)
            scores = jnp.where(live, scores, -jnp.inf)
            weights = jnp.exp(scores - jnp.max(scores, axis=0, keepdims=True))
            total = jnp.sum(weights, axis=0, keepdims=True)
            mixed = contract(value_rows, weights.astype(BF16), 0, 0)
            out[head * HEAD : (head + 1) * HEAD, slot * 256 : (slot + 1) * 256] = (
                mixed / total
            ).astype(BF16)


def fill_out_weight(where, pieces, weight):
    here = lax.rem(where[0], 2) * 4 + where[1] * 2 + where[2]
    block = D // 16
    for code, piece in zip((0, 2, 1, 3), pieces):
        for ez in (0, 1):
            row = jnp.bitwise_xor(here, 4 * ez + code) * block
            for part in (0, 1):
                weight[part, pl.ds(pl.multiple_of(row, 16), block), :] = piece[ez, part]


def merge_kernel(where, *refs):
    parts = refs[:8]
    residual, out_pieces, arrived = refs[8], refs[9:13], refs[13:17]
    keep_out, send_out, heads, out_weight, weight = refs[17:]
    here = where[1] * 2 + where[2]
    fill_out_weight(where, out_pieces, out_weight)
    for code in range(4):
        for ey in (0, 1):
            base = ey * (D // 2) + 2 * HEAD * jnp.bitwise_xor(here, code)
            rows = pl.ds(pl.multiple_of(base, 16), 2 * HEAD)
            for slot in range(4):
                at = (slot ^ code) * 256
                heads[slot, rows, :] = parts[2 * code + ey][:, at : at + 256]
    for steps in range(4):
        weight[z_behind(where[0], steps)] = arrived[steps][...]
    sub_rows = [[], [], [], []]
    for slot in range(4):
        at = slice(slot * 256, (slot + 1) * 256)
        branch = contract(out_weight[0], heads[slot, : D // 2, :], 1, 0) + contract(
            out_weight[1], heads[slot, D // 2 :, :], 1, 0
        )
        after = (residual[:, at].astype(F32) + branch).astype(BF16)
        for sub in range(4):
            sub_rows[sub].append(after[:, sub * 64 : (sub + 1) * 64])
    total = 0.0
    for sub in range(4):
        left = jnp.concatenate([weight[z, sub] for z in range(4)], axis=0)
        total = total + contract(left, jnp.concatenate(sub_rows[sub], axis=1), 1, 0)
    low, high = total[:, :128], total[:, 128:]

    def by_core(value):
        turned = jnp.concatenate([value[:, 64:], value[:, :64]], axis=1)
        return jnp.where(where[2] == 0, value, turned)

    keep_out[...] = by_core(jnp.where(where[3] == 0, low, high))
    send_out[...] = by_core(jnp.where(where[3] == 0, high, low))


def split_kernel(whole, out):
    count = whole.shape[1] // 16
    for at in range(16):
        out[at] = whole[:, at * count : (at + 1) * count]


def weight_kernel(where, own, other, gain, text_weight, token_weight, token_gain, rows):
    block = D // 16
    zeros = jnp.zeros((block, 128 - HEAD), BF16)
    here = where[1] * 2 + where[2]
    for at in range(16):
        low = jnp.where(where[2] == 0, own[at].astype(F32), other[at].astype(F32))
        high = jnp.where(where[2] == 0, other[at].astype(F32), own[at].astype(F32))
        piece = jnp.concatenate([low, high], axis=1).astype(BF16)
        padded = jnp.concatenate(
            [part for k in range(3) for part in (piece[:, k * HEAD : (k + 1) * HEAD], zeros)],
            axis=1,
        )
        text_weight[pl.ds(own_half_first(where, at), block), :] = padded
        z = at // 4
        code = jnp.bitwise_xor(here, at % 4)
        rows[code, z * block : (z + 1) * block, :] = padded
        column = jnp.broadcast_to(gain[:, at * block : (at + 1) * block], (128, block)).T
        token_gain[code, z * block : (z + 1) * block, :] = column
    for code in range(4):
        token_weight[code] = rows[code].T


def text_kernel(where, own, own_y, own_x, corner_low, corner_high, gain, weight, is_text, out):
    own_gain = gain[pl.ds(where[3], 1), :]
    other_gain = gain[pl.ds(1 - where[3], 1), :]
    count = own.shape[1]
    for steps in range(4):
        corner = (corner_low, corner_high)[steps // 2][steps % 2]
        for ex in (0, 1):
            left = (own, own_x)[ex][steps].astype(F32)
            right = (corner if ex else own_y[steps]).astype(F32)
            squares = jnp.sum(left * left, axis=-1, keepdims=True) + jnp.sum(
                right * right, axis=-1, keepdims=True
            )
            scale = lax.rsqrt(squares * (1.0 / D) + eps_norm)
            left = (left * scale * own_gain).astype(BF16)
            right = (right * scale * other_gain).astype(BF16)
            proj = contract(left, weight[: D // 2, :], 1, 0) + contract(
                right, weight[D // 2 :, :], 1, 0
            )
            row = (2 * z_behind(where[0], steps) + jnp.bitwise_xor(where[1], ex)) * count
            at = pl.ds(pl.multiple_of(row, 16), count)
            out[at, :] = jnp.where(is_text[at, :1] > 0.0, proj, 0.0).astype(BF16)


def select_kernel(where, flat_pos, select, is_text):
    positions = flat_pos[...]
    block_rows = select.shape[0] // 8
    for block in range(8):
        first = (2 * block + where[2]) * block_rows
        row = first + lax.broadcasted_iota(jnp.int32, (block_rows, positions.shape[1]), 0)
        hit = jnp.where(row == positions, 1.0, 0.0)
        at = slice(block * block_rows, (block + 1) * block_rows)
        select[at, :] = hit.astype(BF16)
        none = 1.0 - jnp.max(hit, axis=-1, keepdims=True)
        is_text[at, :] = jnp.broadcast_to(none, (block_rows, 128))


def token_columns(parts, sx):
    blocks = []
    for code, (ex, _) in enumerate(FOUR):
        part = parts[2 * code + (sx ^ ex)]
        blocks.append(jnp.concatenate([part[z] for z in range(4)], axis=1))
    return blocks


def place_kernel(*refs):
    parts = refs[:8]
    gain, weight, select, text_proj, query, key_out, value_out, proj = refs[8:]
    for sx in (0, 1):
        blocks = token_columns(parts, sx)
        squares = sum(
            jnp.sum(jnp.square(block.astype(F32)), axis=0, keepdims=True) for block in blocks
        )
        scale = lax.rsqrt(squares * (1.0 / D) + eps_norm)
        total = 0.0
        for at, block in enumerate(blocks):
            normed = (block.astype(F32) * scale * gain[at][:, :1]).astype(BF16)
            total = total + contract(weight[at], normed, 1, 0)
        proj[:, sx * 512 : (sx + 1) * 512] = total.astype(BF16)
    rows = contract(select[...], proj[...], 1, 1) + text_proj[...].astype(F32)
    rows = rows.astype(BF16)
    query[...] = rows[:, :128]
    key_out[...] = rows[:, 128:256]
    value_out[...] = rows[:, 256:]


def route_kernel(where, *refs):
    parts = refs[:8]
    flat_pos, routed = refs[8:]
    positions = flat_pos[...]
    block_rows = routed.shape[1]
    own_block = 4 * where[0] + 2 * where[1] + where[2]
    row = own_block * block_rows + lax.broadcasted_iota(
        jnp.int32, (block_rows, positions.shape[1]), 0
    )
    select = jnp.where(row == positions, 1.0, 0.0).astype(BF16)
    low, high = token_columns(parts, 0), token_columns(parts, 1)
    for at in range(4):
        moved = contract(select[:, :512], low[at], 1, 1) + contract(
            select[:, 512:], high[at], 1, 1
        )
        routed[at] = moved.astype(BF16)


def decode_kernel(where, query, own_key, own_value, other_key, other_value, out):
    rows = query.shape[0] // 8
    later = where[2] > 0
    for block in range(8):
        count = (block + 1) * rows
        asked = query[block * rows : count, :]
        own = contract(asked, own_key[:count, :], 1, 1) * HEAD ** (-0.5)
        other = contract(asked, other_key[:count, :], 1, 1) * HEAD ** (-0.5)
        row = lax.broadcasted_iota(jnp.int32, (rows, count), 0) + block * rows
        column = lax.broadcasted_iota(jnp.int32, (rows, count), 1)
        own = jnp.where(column <= row, own, -jnp.inf)
        limit = jnp.where(later, count, block * rows)
        other = jnp.where(column < limit, other, -jnp.inf)
        best = jnp.maximum(
            jnp.max(own, axis=-1, keepdims=True), jnp.max(other, axis=-1, keepdims=True)
        )
        own = jnp.exp(own - best)
        other = jnp.exp(other - best)
        total = jnp.sum(own, axis=-1, keepdims=True) + jnp.sum(other, axis=-1, keepdims=True)
        mixed = contract(own.astype(BF16), own_value[:count, :], 1, 0) + contract(
            other.astype(BF16), other_value[:count, :], 1, 0
        )
        mixed = (mixed / total).astype(BF16)
        for group in range(rows // 16):
            piece = mixed[group * 16 : (group + 1) * 16, :HEAD]
            for y in (0, 1):
                out[2 * block + y, :, group * HEAD : (group + 1) * HEAD] = piece


def finish_kernel(where, heads, own, at_x, at_c, at_xc, residual, out, weight, sorted_heads):
    fill_out_weight(where, (own, at_x, at_c, at_xc), weight)
    for at in range(16):
        chip, y = at // 2, at % 2
        half = jnp.bitwise_xor(where[3], y)
        for group in range(out.shape[0] // 16):
            sorted_heads[
                half, group * 16 : (group + 1) * 16, chip * HEAD : (chip + 1) * HEAD
            ] = heads[at, :, group * HEAD : (group + 1) * HEAD]
    branch = contract(sorted_heads[0], weight[0], 1, 1) + contract(sorted_heads[1], weight[1], 1, 1)
    out[...] = (residual[...].astype(F32) + branch).astype(BF16)


def run(kernel, shapes, scratch, *operands, scalars=None, grant=GRANT):
    specs = [pl.BlockSpec()] * len(operands)
    if scalars is not None:
        specs, operands = [SMEM] + specs, (scalars,) + operands
    single = not isinstance(shapes, (list, tuple))
    return pl.pallas_call(
        kernel,
        out_shape=shapes,
        in_specs=specs,
        out_specs=pl.BlockSpec() if single else [pl.BlockSpec()] * len(shapes),
        scratch_shapes=scratch,
        compiler_params=pltpu.CompilerParams(vmem_limit_bytes=grant),
    )(*operands)


OUT_Y = [(2 * w + 1 - w // 8, 2 * w + w // 8) for w in range(16)]
OUT_FAR = [(2 * w + w // 8, 2 * (w ^ 8) + w // 8) for w in range(16)]
OUT_NEAR = [(w, w ^ 4) for w in range(16)]


def send_out_y(turned):
    return lax.ppermute(turned, ("wide", "narrow"), OUT_Y)


def send_out_far(both):
    return lax.ppermute(both, ("wide", "narrow"), OUT_FAR)


def send_out_near(held):
    return lax.ppermute(held, "wide", OUT_NEAR)


def out_over_y(turned):
    return jnp.stack([turned, send_out_y(turned)])


def out_over_far(both, z, y):
    return jnp.where(z // 2 == y, both, send_out_far(both))


def out_over_near(held):
    return jnp.stack([held, send_out_near(held)])


def fence(*values):
    return lax.optimization_barrier(values)


def shards_fast(
    patches,
    grid,
    vit_gain,
    vit_qkv,
    vit_out,
    merge_weight,
    text_embeds,
    prompt_pos,
    dec_gain,
    dec_qkv,
    dec_out,
):
    w = lax.axis_index("wide").astype(jnp.int32)
    y = lax.axis_index("narrow").astype(jnp.int32)
    z, x, c = w // 4, (w // 2) % 2, w % 2
    where = jnp.stack([z, x, c, y])
    half = D // 2
    text_rows = text_embeds.shape[0]

    columns = vit_qkv.shape[1] // 4
    sliced = vit_qkv.reshape(-1, 2, 2, columns).transpose(1, 2, 0, 3)
    sliced = jnp.pad(sliced, ((0, 0), (0, 0), (0, 0), (0, 512 - columns)))

    def halves(value, bit):
        own = lax.dynamic_index_in_dim(value, bit, 0, keepdims=False)
        return own, lax.dynamic_index_in_dim(value, 1 - bit, 0, keepdims=False)

    own_cols, sent_cols = halves(sliced, x)
    merge_first = merge_weight.transpose(0, 2, 1)
    patch, sent_cols = fence(patches[0], sent_cols)
    came_cols, patch_y, merge_second, out_held = fence(
        over_x(sent_cols), over_y(patch), next_z(merge_first), out_over_y(vit_out.T)
    )
    own_cols, sent_cols = halves(jnp.stack([own_cols, came_cols], axis=-3), c)
    patch, sent_cols = fence(patch, sent_cols)
    sliced = jnp.stack([own_cols, over_c(sent_cols)], axis=-3).reshape(-1, 512)
    second, patch_x, out_held = fence(
        next_z(sliced), over_x(patch), out_over_far(out_held, z, y)
    )
    patch_xy = over_xy(patch)
    third, patch_xy, out_held, text_first = fence(
        next_z(second), patch_xy, out_over_near(out_held), text_embeds
    )
    patch_parts = [patch, patch_y, over_c(patch), over_c(patch_y), patch_x, patch_xy]
    patch_parts += [over_c(patch_x), over_c(patch_xy)]
    codes = jnp.arange(4, dtype=jnp.int32)
    live = prompt_pos[4 * z + jnp.bitwise_xor(2 * x + c, codes)] >= 0
    live = jnp.tile(live.astype(F32).T, (4, 1))
    rows = 4 * patches.shape[1]
    normed, residual = run(
        norm_kernel,
        [jax.ShapeDtypeStruct((rows, D), BF16), jax.ShapeDtypeStruct((half, rows), BF16)],
        [],
        *patch_parts,
        vit_gain.reshape(2, half),
        scalars=where,
        grant=MOST,
    )
    fourth, normed, out_x, out_c, text_second, merge_second, live = fence(
        next_z(third),
        normed,
        over_x(out_held),
        over_c(out_held),
        next_z(text_first),
        merge_second,
        live,
    )
    out_pieces = [out_held, out_x, out_c, over_c(out_x)]
    vit_weight = [sliced, second, third, fourth]
    merge_third = next_z(merge_second)
    attended = run(
        encode_kernel,
        jax.ShapeDtypeStruct((2 * HEAD, rows), BF16),
        [pltpu.VMEM((D, 512), BF16)],
        normed,
        *vit_weight,
        live,
        scalars=where,
    )
    attended, merge_third = fence(attended, merge_third)
    merge_fourth = next_z(merge_third)
    text_third = next_z(text_second)
    att_y, att_x, att_xy, merge_fourth, text_fourth, dec_qkv, turned = fence(
        over_y(attended),
        over_x(attended),
        over_xy(attended),
        merge_fourth,
        next_z(text_third),
        dec_qkv,
        dec_out.T,
    )
    head_parts = [attended, att_y, over_c(attended), over_c(att_y), att_x, att_xy]
    head_parts += [over_c(att_x), over_c(att_xy)]
    pieces = run(
        split_kernel,
        jax.ShapeDtypeStruct((16, dec_qkv.shape[0], dec_qkv.shape[1] // 16), BF16),
        [],
        dec_qkv,
    )
    pieces = lax.all_to_all(pieces, "wide", 0, 0, tiled=True)
    merge_rows = [merge_first, merge_second, merge_third, merge_fourth]
    part = jax.ShapeDtypeStruct((320, 128), F32)
    kept, sent = run(
        merge_kernel,
        [part, part],
        [
            pltpu.VMEM((4, D, 256), BF16),
            pltpu.VMEM((2, half, half), BF16),
            pltpu.VMEM((4,) + merge_first.shape, BF16),
        ],
        *head_parts,
        residual,
        *out_pieces,
        *merge_rows,
        scalars=where,
        grant=MOST,
    )
    stacked = jnp.stack([text_embeds, text_second, text_third, text_fourth])
    kept, sent, pieces, dec_came, text_y, text_x = fence(
        kept, sent, pieces, send_out_y(turned), over_y(stacked), over_x(stacked)
    )
    came = over_y(sent)
    text_weight, token_weight, token_gain = run(
        weight_kernel,
        [
            jax.ShapeDtypeStruct((D, 384), BF16),
            jax.ShapeDtypeStruct((4, 384, D // 4), BF16),
            jax.ShapeDtypeStruct((4, D // 4, 128), F32),
        ],
        [pltpu.VMEM((4, D // 4, 384), BF16)],
        pieces,
        over_c(pieces),
        dec_gain[None],
        scalars=where,
    )
    merged = (kept + came).astype(BF16)
    merged, text_y, text_x = fence(merged, text_y, text_x)
    sx = jnp.arange(2, dtype=jnp.int32)[:, None, None]
    k = jnp.arange(4, dtype=jnp.int32)[None, :, None]
    sc = jnp.arange(2, dtype=jnp.int32)[None, None, :]
    image = 4 * ((z + 4 - k) % 4) + 2 * (sx ^ x ^ y) + sc
    flat_pos = prompt_pos[image.reshape(-1)].reshape(1, -1)
    select, is_text = run(
        select_kernel,
        [
            jax.ShapeDtypeStruct((8 * text_rows, flat_pos.shape[1]), BF16),
            jax.ShapeDtypeStruct((8 * text_rows, 128), F32),
        ],
        [],
        flat_pos,
        scalars=where,
    )

    def project_text(text_y, text_x, corner):
        return run(
            text_kernel,
            jax.ShapeDtypeStruct((8 * text_rows, 384), BF16),
            [],
            stacked,
            text_y,
            text_x,
            *corner,
            dec_gain.reshape(2, half),
            text_weight,
            is_text,
            scalars=where,
        )

    dec_both = jnp.stack([turned, dec_came])
    *tokens, dec_came = fence(*around_z(merged), send_out_far(dec_both))
    dec_held = jnp.where(z // 2 == y, dec_both, dec_came)
    tokens = jnp.stack(tokens)
    corner = [over_y(text_x[:2]), over_x(text_y[2:])]
    text_proj = project_text(text_y, text_x, corner)
    token_y, token_x, token_xy, text_proj, dec_came = fence(
        over_y(tokens), over_x(tokens), over_xy(tokens), text_proj, send_out_near(dec_held)
    )
    dec_held = jnp.stack([dec_held, dec_came])
    token_parts = [tokens, token_y, over_c(tokens), over_c(token_y)]
    token_parts += [token_x, token_xy, over_c(token_x), over_c(token_xy)]

    lanes = jax.ShapeDtypeStruct((8 * text_rows, 128), BF16)
    query, key, value = run(
        place_kernel,
        [lanes, lanes, lanes],
        [pltpu.VMEM((384, 1024), BF16)],
        *token_parts,
        token_gain,
        token_weight,
        select,
        text_proj,
    )
    heads = run(
        decode_kernel,
        jax.ShapeDtypeStruct((16, 16, text_rows // 16 * HEAD), BF16),
        [],
        query,
        key,
        value,
        over_c(key),
        over_c(value),
        scalars=where,
    )
    heads, dec_x, dec_c = fence(heads, over_x(dec_held), over_c(dec_held))
    by_core = [[2 * w_ + y_ for w_ in range(c_, 16, 2) for y_ in (0, 1)] for c_ in (0, 1)]
    heads = lax.all_to_all(
        heads, ("wide", "narrow"), 0, 0, axis_index_groups=by_core, tiled=True
    )
    routed = run(
        route_kernel,
        jax.ShapeDtypeStruct((4, text_rows, 320), BF16),
        [],
        *token_parts,
        flat_pos,
        scalars=where,
    )
    routed = routed.reshape(4, text_rows, 4, D // 16)
    routed = lax.dynamic_slice_in_dim(routed, 2 * y, 2, axis=2)
    ordered = jnp.stack(
        [
            lax.dynamic_index_in_dim(routed, jnp.bitwise_xor(2 * x + c, code), 0, keepdims=False)
            for code in range(4)
        ]
    )
    ordered = ordered.transpose(1, 2, 0, 3).reshape(text_rows, half)
    mine = w * text_rows + jnp.arange(text_rows, dtype=jnp.int32)
    is_image = jnp.any(mine[:, None] == prompt_pos.reshape(1, -1), axis=1)
    dec_in = jnp.where(is_image[:, None], ordered, text_embeds)
    return run(
        finish_kernel,
        jax.ShapeDtypeStruct(text_embeds.shape, BF16),
        [
            pltpu.VMEM((2, half, half), BF16),
            pltpu.VMEM((2, text_rows, half), BF16),
        ],
        heads,
        dec_held,
        dec_x,
        dec_c,
        over_c(dec_x),
        dec_in,
        scalars=where,
    )


def solution(mesh):
    placed = (
        P("wide", None, "narrow"),
        P("wide", None),
        P(),
        P("wide", "narrow"),
        P("narrow", "wide"),
        P(None, "narrow", "wide"),
        P("wide", "narrow"),
        P(),
        P(),
        P("wide", "narrow"),
        P("narrow", "wide"),
    )
    sizes = (mesh.shape["wide"], mesh.shape["narrow"])
    shards = shards_fast if sizes == (16, 2) else shards_any
    return jax.shard_map(
        shards, mesh=mesh, in_specs=placed, out_specs=P("wide", "narrow"), check_vma=False
    )
```

```python
import jax
import jax.numpy as jnp
from jax import lax
from jax.experimental import pallas as pl
from jax.experimental.pallas import tpu as pltpu
from jax.sharding import PartitionSpec as P

D = 1280
HEAD = 80
PATCH_SIDE = 16


eps_norm = 1e-06


def layer_norm(values, gain):
    center = values - jnp.mean(values, axis=-1, keepdims=True)
    spread = jnp.mean(center * center, axis=-1, keepdims=True)
    return center * lax.rsqrt(spread + eps_norm) * gain


def rms_norm(values, gain):
    return values * lax.rsqrt(jnp.mean(values * values, axis=-1, keepdims=True) + eps_norm) * gain


def add_rows(left, piece):
    return jnp.dot(left, piece, preferred_element_type=jnp.float32)


def image_attention(query, keys, values, keep):
    scores = jnp.einsum(
        "iqhd,ikhd->ihqk", query, keys, preferred_element_type=jnp.float32
    ) * HEAD ** (-0.5)
    scores = jnp.where(keep[:, None, None, :], scores, -jnp.inf)
    weights = jnp.exp(scores - jnp.max(scores, axis=-1, keepdims=True))
    total = jnp.sum(weights, axis=-1)
    mixed = jnp.einsum(
        "ihqk,ikhd->iqhd", weights.astype(jnp.bfloat16), values, preferred_element_type=jnp.float32
    )
    return (mixed / jnp.transpose(total, (0, 2, 1))[..., None]).astype(jnp.bfloat16)


def attend(state, query, query_pos, keys, values, key_pos):
    best, total, summed = state
    scores = jnp.einsum("qhd,khd->hqk", query, keys, preferred_element_type=jnp.float32) * HEAD ** (
        -0.5
    )
    allowed = key_pos[None, :] <= query_pos[:, None]
    scores = jnp.where(allowed[None], scores, -jnp.inf)
    new_best = jnp.maximum(best, jnp.max(scores, axis=-1))
    shift = jnp.where(jnp.isfinite(new_best), new_best, 0.0)
    weights = jnp.exp(scores - shift[..., None])
    fade = jnp.exp(best - shift)
    total = total * fade + jnp.sum(weights, axis=-1)
    update = jnp.einsum(
        "hqk,khd->hqd", weights.astype(jnp.bfloat16), values, preferred_element_type=jnp.float32
    )
    summed = summed * fade[..., None] + update
    return (new_best, total, summed)


def fresh_state(heads, count):
    return (
        jnp.full((heads, count), -jnp.inf, jnp.float32),
        jnp.zeros((heads, count), jnp.float32),
        jnp.zeros((heads, count, HEAD), jnp.float32),
    )


def finish(state):
    best, total, summed = state
    return summed / total[..., None]


def shards_any(
    patches,
    grid,
    vit_gain,
    vit_qkv,
    vit_out,
    merge_weight,
    text_embeds,
    prompt_pos,
    dec_gain,
    dec_qkv,
    dec_out,
):
    images, slots, part_width = patches.shape
    side = PATCH_SIDE
    half_side = side // 2
    rows_vit = images * slots
    local_heads = vit_qkv.shape[1] // (3 * HEAD)
    whole = lax.all_gather(patches, "narrow", axis=2, tiled=True)
    normed = (
        layer_norm(whole.astype(jnp.float32), vit_gain).astype(jnp.bfloat16).reshape(rows_vit, D)
    )
    projected = add_rows(normed, lax.all_gather(vit_qkv, "wide", axis=0, tiled=True))
    projected = projected.astype(jnp.bfloat16).reshape(images, slots, local_heads, 3, HEAD)
    slot_ids = jnp.arange(slots, dtype=jnp.int32)
    keep = ((slot_ids // side)[None, :] < grid[:, 0:1]) & (
        (slot_ids % side)[None, :] < grid[:, 1:2]
    )
    attended = image_attention(
        projected[:, :, :, 0], projected[:, :, :, 1], projected[:, :, :, 2], keep
    )
    attended = attended.reshape(rows_vit, local_heads * HEAD)
    vit_partial = jnp.dot(
        attended,
        lax.all_gather(vit_out, "wide", axis=1, tiled=True),
        preferred_element_type=jnp.float32,
    )
    vit_branch = lax.psum_scatter(vit_partial, "narrow", scatter_dimension=1, tiled=True)
    after = (patches.reshape(rows_vit, part_width).astype(jnp.float32) + vit_branch).astype(
        jnp.bfloat16
    )
    grouped = after.reshape(images, half_side, 2, half_side, 2, part_width).transpose(
        0, 1, 3, 2, 4, 5
    )
    grouped = grouped.reshape(images * half_side * half_side, 4 * part_width)
    piece = lax.all_gather(merge_weight, "wide", axis=2, tiled=True)
    flat_piece = piece.reshape(4 * part_width, piece.shape[2])
    merge_partial = jnp.dot(grouped, flat_piece, preferred_element_type=jnp.float32)
    merged = lax.psum_scatter(merge_partial, "narrow", scatter_dimension=1, tiled=True).astype(
        jnp.bfloat16
    )
    text_rows = text_embeds.shape[0]
    half_rows = text_rows // 2
    wide_index = lax.axis_index("wide")
    offsets = jnp.arange(text_rows, dtype=jnp.int32)
    mine = wide_index * text_rows + offsets
    flat_pos = prompt_pos.reshape(-1)
    select = (mine[:, None] == flat_pos[None, :]).astype(jnp.bfloat16)
    routed = jnp.dot(
        select,
        lax.all_gather(merged, "wide", axis=0, tiled=True),
        preferred_element_type=jnp.float32,
    )
    is_image = jnp.any(mine[:, None] == flat_pos[None, :], axis=1)
    dec_in = jnp.where(is_image[:, None], routed.astype(jnp.bfloat16), text_embeds)
    dec_whole = lax.all_gather(dec_in, "narrow", axis=1, tiled=True)
    dec_normed = rms_norm(dec_whole.astype(jnp.float32), dec_gain).astype(jnp.bfloat16)
    dec_proj = add_rows(dec_normed, lax.all_gather(dec_qkv, "wide", axis=0, tiled=True))
    dec_proj = dec_proj.astype(jnp.bfloat16).reshape(text_rows, local_heads, 3, HEAD)
    queries = dec_proj[:, :, 0]
    keys = dec_proj[:, :, 1].reshape(text_rows, local_heads * HEAD)
    values = dec_proj[:, :, 2].reshape(text_rows, local_heads * HEAD)
    low_pos = mine[:half_rows]
    high_pos = mine[half_rows:]
    low_query = queries[:half_rows]
    high_query = queries[half_rows:]
    start_state = (
        fresh_state(local_heads, half_rows),
        fresh_state(local_heads, text_rows - half_rows),
    )
    key_piece = lax.all_gather(keys, "wide", axis=0, tiled=True)
    value_piece = lax.all_gather(values, "wide", axis=0, tiled=True)
    count = key_piece.shape[0]
    span_rows = count
    while span_rows > 2048 and span_rows % 2 == 0:
        span_rows = span_rows // 2
    key_heads = key_piece.reshape(count, local_heads, HEAD)
    value_heads = value_piece.reshape(count, local_heads, HEAD)

    def one_span(index, carry):
        begin = (index * span_rows).astype(jnp.int32)
        key_span = lax.dynamic_slice_in_dim(key_heads, begin, span_rows)
        value_span = lax.dynamic_slice_in_dim(value_heads, begin, span_rows)
        key_pos = begin + jnp.arange(span_rows, dtype=jnp.int32)
        earliest = jnp.min(key_pos)
        first = lax.cond(
            earliest <= jnp.max(low_pos),
            lambda inner: attend(inner, low_query, low_pos, key_span, value_span, key_pos),
            lambda inner: inner,
            carry[0],
        )
        second = lax.cond(
            earliest <= jnp.max(high_pos),
            lambda inner: attend(inner, high_query, high_pos, key_span, value_span, key_pos),
            lambda inner: inner,
            carry[1],
        )
        return (first, second)

    final = lax.fori_loop(0, count // span_rows, one_span, start_state)
    heads_out = jnp.concatenate([finish(final[0]), finish(final[1])], axis=1)
    heads_out = (
        heads_out.transpose(1, 0, 2).reshape(text_rows, local_heads * HEAD).astype(jnp.bfloat16)
    )
    dec_partial = jnp.dot(
        heads_out,
        lax.all_gather(dec_out, "wide", axis=1, tiled=True),
        preferred_element_type=jnp.float32,
    )
    dec_branch = lax.psum_scatter(
        dec_partial.astype(jnp.bfloat16), "narrow", scatter_dimension=1, tiled=True
    ).astype(jnp.float32)
    result = (dec_in.astype(jnp.float32) + dec_branch).astype(jnp.bfloat16)
    return result


CROSS_X = [(w, w ^ 2) for w in range(16)]
CROSS_C = [(w, w ^ 1) for w in range(16)]
CROSS_Y = [(0, 1), (1, 0)]
GROUPS_Z = [[b, 4 + b, 8 + b, 12 + b] for b in range(4)]
GROUPS_B = [[4 * z + b for b in range(4)] for z in range(4)]
FOUR = ((0, 0), (0, 1), (1, 0), (1, 1))
SMEM = pl.BlockSpec(memory_space=pltpu.SMEM)
F32 = jnp.float32
BF16 = jnp.bfloat16
GRANT = 48 * 1024 * 1024
MOST = 59 * 1024 * 1024


def over_x(value):
    return lax.ppermute(value, "wide", CROSS_X)


def over_c(value):
    return lax.ppermute(value, "wide", CROSS_C)


def over_y(value):
    return lax.ppermute(value, "narrow", CROSS_Y)


RING_Z = [(4 * a + b, 4 * n + b) for a, n in ((0, 1), (1, 3), (3, 2), (2, 0)) for b in range(4)]


def next_z(value):
    return lax.ppermute(value, "wide", RING_Z)


def z_behind(z, steps):
    place = lax.rem(jnp.bitwise_xor(z, z // 2) + 4 - steps, 4)
    return jnp.bitwise_xor(place, place // 2)


def around_z(value):
    return [value] + [
        lax.ppermute(value, "wide", [(w, (w + 4 * k) % 16) for w in range(16)]) for k in (1, 2, 3)
    ]


def over_xy(value):
    both = [(2 * w + y, 2 * (w ^ 2) + 1 - y) for w in range(16) for y in (0, 1)]
    return lax.ppermute(value, ("wide", "narrow"), both)


def share_xy(value):
    return [[value, over_y(value)], [over_x(value), over_xy(value)]]


def share_xyc(value):
    pieces = share_xy(value)
    return [
        over_c(pieces[ex][ey]) if ec else pieces[ex][ey]
        for ex, ec in FOUR
        for ey in (0, 1)
    ]


def contract(left, right, left_dim, right_dim):
    return lax.dot_general(
        left, right, (((left_dim,), (right_dim,)), ((), ())), preferred_element_type=F32
    )


def patch_order():
    row = lax.broadcasted_iota(jnp.int32, (256, 256), 0)
    column = lax.broadcasted_iota(jnp.int32, (256, 256), 1)
    sub, token = row // 64, row % 64
    source = (2 * (token // 8) + sub // 2) * 16 + 2 * (token % 8) + sub % 2
    return jnp.where(column == source, 1.0, 0.0).astype(BF16)


def norm_kernel(where, *refs):
    parts = refs[:8]
    gain, normed, residual = refs[8:]
    order = patch_order()
    own_gain = gain[pl.ds(where[3], 1), :]
    other_gain = gain[pl.ds(1 - where[3], 1), :]
    for slot in range(4):
        raw = parts[2 * slot][...]
        own = raw.astype(F32)
        other = parts[2 * slot + 1][...].astype(F32)
        mean = (
            jnp.sum(own, axis=-1, keepdims=True) + jnp.sum(other, axis=-1, keepdims=True)
        ) * (1.0 / D)
        own = own - mean
        other = other - mean
        spread = (
            jnp.sum(own * own, axis=-1, keepdims=True)
            + jnp.sum(other * other, axis=-1, keepdims=True)
        ) * (1.0 / D)
        scale = lax.rsqrt(spread + eps_norm)
        own = (own * scale * own_gain).astype(BF16)
        other = (other * scale * other_gain).astype(BF16)
        at = slice(slot * 256, (slot + 1) * 256)
        normed[at, : D // 2] = contract(order, own, 1, 0).astype(BF16)
        normed[at, D // 2 :] = contract(order, other, 1, 0).astype(BF16)
        residual[:, at] = contract(raw, order, 0, 1).astype(BF16)


def own_half_first(where, block):
    row = block * (D // 16) - where[3] * (D // 2)
    return pl.multiple_of(jnp.where(row < 0, row + D, row), 16)


def encode_kernel(where, normed, first, second, third, fourth, keep, out, weight):
    block = D // 16
    here = where[1] * 2 + where[2]
    for steps, piece in enumerate((first, second, third, fourth)):
        z = z_behind(where[0], steps)
        for code in range(4):
            row = own_half_first(where, 4 * z + jnp.bitwise_xor(here, code))
            weight[pl.ds(row, block), :] = piece[code * block : (code + 1) * block, :]
    for slot in range(4):
        proj = contract(normed[slot * 256 : (slot + 1) * 256, :], weight[...], 1, 0).astype(BF16)
        live = keep[:, slot : slot + 1] > 0.0
        for head in (0, 1):
            base = head * 3 * HEAD
            query = proj[:, base : base + HEAD]
            key_rows = proj[:, base + HEAD : base + 2 * HEAD]
            value_rows = proj[:, base + 2 * HEAD : base + 3 * HEAD]
            scores = contract(key_rows, query, 1, 1) * HEAD ** (-0.5)
            scores = jnp.where(live, scores, -jnp.inf)
            weights = jnp.exp(scores - jnp.max(scores, axis=0, keepdims=True))
            total = jnp.sum(weights, axis=0, keepdims=True)
            mixed = contract(value_rows, weights.astype(BF16), 0, 0)
            out[head * HEAD : (head + 1) * HEAD, slot * 256 : (slot + 1) * 256] = (
                mixed / total
            ).astype(BF16)


def fill_out_weight(where, pieces, weight):
    here = lax.rem(where[0], 2) * 4 + where[1] * 2 + where[2]
    block = D // 16
    for code, piece in zip((0, 2, 1, 3), pieces):
        for ez in (0, 1):
            row = jnp.bitwise_xor(here, 4 * ez + code) * block
            for part in (0, 1):
                weight[part, pl.ds(pl.multiple_of(row, 16), block), :] = piece[ez, part]


def merge_kernel(where, *refs):
    parts = refs[:8]
    residual, out_pieces, arrived = refs[8], refs[9:13], refs[13:17]
    keep_out, send_out, heads, out_weight, weight = refs[17:]
    here = where[1] * 2 + where[2]
    fill_out_weight(where, out_pieces, out_weight)
    for code in range(4):
        for ey in (0, 1):
            base = ey * (D // 2) + 2 * HEAD * jnp.bitwise_xor(here, code)
            rows = pl.ds(pl.multiple_of(base, 16), 2 * HEAD)
            for slot in range(4):
                at = (slot ^ code) * 256
                heads[slot, rows, :] = parts[2 * code + ey][:, at : at + 256]
    for steps in range(4):
        weight[z_behind(where[0], steps)] = arrived[steps][...]
    sub_rows = [[], [], [], []]
    for slot in range(4):
        at = slice(slot * 256, (slot + 1) * 256)
        branch = contract(out_weight[0], heads[slot, : D // 2, :], 1, 0) + contract(
            out_weight[1], heads[slot, D // 2 :, :], 1, 0
        )
        after = (residual[:, at].astype(F32) + branch).astype(BF16)
        for sub in range(4):
            sub_rows[sub].append(after[:, sub * 64 : (sub + 1) * 64])
    total = 0.0
    for sub in range(4):
        left = jnp.concatenate([weight[z, sub] for z in range(4)], axis=0)
        total = total + contract(left, jnp.concatenate(sub_rows[sub], axis=1), 1, 0)
    low, high = total[:, :128], total[:, 128:]

    def by_core(value):
        turned = jnp.concatenate([value[:, 64:], value[:, :64]], axis=1)
        return jnp.where(where[2] == 0, value, turned)

    keep_out[...] = by_core(jnp.where(where[3] == 0, low, high))
    send_out[...] = by_core(jnp.where(where[3] == 0, high, low))


def split_kernel(whole, out):
    count = whole.shape[1] // 16
    for at in range(16):
        out[at] = whole[:, at * count : (at + 1) * count]


def weight_kernel(where, own, other, gain, text_weight, token_weight, token_gain, rows):
    block = D // 16
    zeros = jnp.zeros((block, 128 - HEAD), BF16)
    here = where[1] * 2 + where[2]
    for at in range(16):
        low = jnp.where(where[2] == 0, own[at].astype(F32), other[at].astype(F32))
        high = jnp.where(where[2] == 0, other[at].astype(F32), own[at].astype(F32))
        piece = jnp.concatenate([low, high], axis=1).astype(BF16)
        padded = jnp.concatenate(
            [part for k in range(3) for part in (piece[:, k * HEAD : (k + 1) * HEAD], zeros)],
            axis=1,
        )
        text_weight[pl.ds(own_half_first(where, at), block), :] = padded
        z = at // 4
        code = jnp.bitwise_xor(here, at % 4)
        rows[code, z * block : (z + 1) * block, :] = padded
        column = jnp.broadcast_to(gain[:, at * block : (at + 1) * block], (128, block)).T
        token_gain[code, z * block : (z + 1) * block, :] = column
    for code in range(4):
        token_weight[code] = rows[code].T


def text_kernel(where, own, own_y, own_x, corner_low, corner_high, gain, weight, is_text, out):
    own_gain = gain[pl.ds(where[3], 1), :]
    other_gain = gain[pl.ds(1 - where[3], 1), :]
    count = own.shape[1]
    for steps in range(4):
        corner = (corner_low, corner_high)[steps // 2][steps % 2]
        for ex in (0, 1):
            left = (own, own_x)[ex][steps].astype(F32)
            right = (corner if ex else own_y[steps]).astype(F32)
            squares = jnp.sum(left * left, axis=-1, keepdims=True) + jnp.sum(
                right * right, axis=-1, keepdims=True
            )
            scale = lax.rsqrt(squares * (1.0 / D) + eps_norm)
            left = (left * scale * own_gain).astype(BF16)
            right = (right * scale * other_gain).astype(BF16)
            proj = contract(left, weight[: D // 2, :], 1, 0) + contract(
                right, weight[D // 2 :, :], 1, 0
            )
            row = (2 * z_behind(where[0], steps) + jnp.bitwise_xor(where[1], ex)) * count
            at = pl.ds(pl.multiple_of(row, 16), count)
            out[at, :] = jnp.where(is_text[at, :1] > 0.0, proj, 0.0).astype(BF16)


def select_kernel(where, flat_pos, select, is_text):
    positions = flat_pos[...]
    block_rows = select.shape[0] // 8
    for block in range(8):
        first = (2 * block + where[2]) * block_rows
        row = first + lax.broadcasted_iota(jnp.int32, (block_rows, positions.shape[1]), 0)
        hit = jnp.where(row == positions, 1.0, 0.0)
        at = slice(block * block_rows, (block + 1) * block_rows)
        select[at, :] = hit.astype(BF16)
        none = 1.0 - jnp.max(hit, axis=-1, keepdims=True)
        is_text[at, :] = jnp.broadcast_to(none, (block_rows, 128))


def token_columns(parts, sx):
    blocks = []
    for code, (ex, _) in enumerate(FOUR):
        part = parts[2 * code + (sx ^ ex)]
        blocks.append(jnp.concatenate([part[z] for z in range(4)], axis=1))
    return blocks


def place_kernel(*refs):
    parts = refs[:8]
    gain, weight, select, text_proj, query, key_out, value_out, proj = refs[8:]
    for sx in (0, 1):
        blocks = token_columns(parts, sx)
        squares = sum(
            jnp.sum(jnp.square(block.astype(F32)), axis=0, keepdims=True) for block in blocks
        )
        scale = lax.rsqrt(squares * (1.0 / D) + eps_norm)
        total = 0.0
        for at, block in enumerate(blocks):
            normed = (block.astype(F32) * scale * gain[at][:, :1]).astype(BF16)
            total = total + contract(weight[at], normed, 1, 0)
        proj[:, sx * 512 : (sx + 1) * 512] = total.astype(BF16)
    rows = contract(select[...], proj[...], 1, 1) + text_proj[...].astype(F32)
    rows = rows.astype(BF16)
    query[...] = rows[:, :128]
    key_out[...] = rows[:, 128:256]
    value_out[...] = rows[:, 256:]


def route_kernel(where, *refs):
    parts = refs[:8]
    flat_pos, routed = refs[8:]
    positions = flat_pos[...]
    block_rows = routed.shape[1]
    own_block = 4 * where[0] + 2 * where[1] + where[2]
    row = own_block * block_rows + lax.broadcasted_iota(
        jnp.int32, (block_rows, positions.shape[1]), 0
    )
    select = jnp.where(row == positions, 1.0, 0.0).astype(BF16)
    low, high = token_columns(parts, 0), token_columns(parts, 1)
    for at in range(4):
        moved = contract(select[:, :512], low[at], 1, 1) + contract(
            select[:, 512:], high[at], 1, 1
        )
        routed[at] = moved.astype(BF16)


def decode_kernel(where, query, own_key, own_value, other_key, other_value, out):
    rows = query.shape[0] // 8
    later = where[2] > 0
    for block in range(8):
        count = (block + 1) * rows
        asked = query[block * rows : count, :]
        own = contract(asked, own_key[:count, :], 1, 1) * HEAD ** (-0.5)
        other = contract(asked, other_key[:count, :], 1, 1) * HEAD ** (-0.5)
        row = lax.broadcasted_iota(jnp.int32, (rows, count), 0) + block * rows
        column = lax.broadcasted_iota(jnp.int32, (rows, count), 1)
        own = jnp.where(column <= row, own, -jnp.inf)
        limit = jnp.where(later, count, block * rows)
        other = jnp.where(column < limit, other, -jnp.inf)
        best = jnp.maximum(
            jnp.max(own, axis=-1, keepdims=True), jnp.max(other, axis=-1, keepdims=True)
        )
        own = jnp.exp(own - best)
        other = jnp.exp(other - best)
        total = jnp.sum(own, axis=-1, keepdims=True) + jnp.sum(other, axis=-1, keepdims=True)
        mixed = contract(own.astype(BF16), own_value[:count, :], 1, 0) + contract(
            other.astype(BF16), other_value[:count, :], 1, 0
        )
        mixed = (mixed / total).astype(BF16)
        for group in range(rows // 16):
            piece = mixed[group * 16 : (group + 1) * 16, :HEAD]
            for y in (0, 1):
                out[2 * block + y, :, group * HEAD : (group + 1) * HEAD] = piece


def finish_kernel(where, heads, own, at_x, at_c, at_xc, residual, out, weight, sorted_heads):
    fill_out_weight(where, (own, at_x, at_c, at_xc), weight)
    for at in range(16):
        chip, y = at // 2, at % 2
        half = jnp.bitwise_xor(where[3], y)
        for group in range(out.shape[0] // 16):
            sorted_heads[
                half, group * 16 : (group + 1) * 16, chip * HEAD : (chip + 1) * HEAD
            ] = heads[at, :, group * HEAD : (group + 1) * HEAD]
    branch = contract(sorted_heads[0], weight[0], 1, 1) + contract(sorted_heads[1], weight[1], 1, 1)
    out[...] = (residual[...].astype(F32) + branch).astype(BF16)


def run(kernel, shapes, scratch, *operands, scalars=None, grant=GRANT):
    specs = [pl.BlockSpec()] * len(operands)
    if scalars is not None:
        specs, operands = [SMEM] + specs, (scalars,) + operands
    single = not isinstance(shapes, (list, tuple))
    return pl.pallas_call(
        kernel,
        out_shape=shapes,
        in_specs=specs,
        out_specs=pl.BlockSpec() if single else [pl.BlockSpec()] * len(shapes),
        scratch_shapes=scratch,
        compiler_params=pltpu.CompilerParams(vmem_limit_bytes=grant),
    )(*operands)


OUT_Y = [(2 * w + 1 - w // 8, 2 * w + w // 8) for w in range(16)]
OUT_FAR = [(2 * w + w // 8, 2 * (w ^ 8) + w // 8) for w in range(16)]
OUT_NEAR = [(w, w ^ 4) for w in range(16)]


def send_out_y(turned):
    return lax.ppermute(turned, ("wide", "narrow"), OUT_Y)


def send_out_far(both):
    return lax.ppermute(both, ("wide", "narrow"), OUT_FAR)


def send_out_near(held):
    return lax.ppermute(held, "wide", OUT_NEAR)


def out_over_y(turned):
    return jnp.stack([turned, send_out_y(turned)])


def out_over_far(both, z, y):
    return jnp.where(z // 2 == y, both, send_out_far(both))


def out_over_near(held):
    return jnp.stack([held, send_out_near(held)])


def fence(*values):
    return lax.optimization_barrier(values)


def shards_fast(
    patches,
    grid,
    vit_gain,
    vit_qkv,
    vit_out,
    merge_weight,
    text_embeds,
    prompt_pos,
    dec_gain,
    dec_qkv,
    dec_out,
):
    w = lax.axis_index("wide").astype(jnp.int32)
    y = lax.axis_index("narrow").astype(jnp.int32)
    z, x, c = w // 4, (w // 2) % 2, w % 2
    where = jnp.stack([z, x, c, y])
    half = D // 2
    text_rows = text_embeds.shape[0]

    columns = vit_qkv.shape[1] // 4
    sliced = vit_qkv.reshape(-1, 2, 2, columns).transpose(1, 2, 0, 3)
    sliced = jnp.pad(sliced, ((0, 0), (0, 0), (0, 0), (0, 512 - columns)))

    def halves(value, bit):
        own = lax.dynamic_index_in_dim(value, bit, 0, keepdims=False)
        return own, lax.dynamic_index_in_dim(value, 1 - bit, 0, keepdims=False)

    own_cols, sent_cols = halves(sliced, x)
    merge_first = merge_weight.transpose(0, 2, 1)
    patch, sent_cols = fence(patches[0], sent_cols)
    came_cols, patch_y, merge_second, out_held = fence(
        over_x(sent_cols), over_y(patch), next_z(merge_first), out_over_y(vit_out.T)
    )
    own_cols, sent_cols = halves(jnp.stack([own_cols, came_cols], axis=-3), c)
    patch, sent_cols = fence(patch, sent_cols)
    sliced = jnp.stack([own_cols, over_c(sent_cols)], axis=-3).reshape(-1, 512)
    second, patch_x, out_held = fence(
        next_z(sliced), over_x(patch), out_over_far(out_held, z, y)
    )
    patch_xy = over_xy(patch)
    third, patch_xy, out_held, text_first = fence(
        next_z(second), patch_xy, out_over_near(out_held), text_embeds
    )
    patch_parts = [patch, patch_y, over_c(patch), over_c(patch_y), patch_x, patch_xy]
    patch_parts += [over_c(patch_x), over_c(patch_xy)]
    codes = jnp.arange(4, dtype=jnp.int32)
    live = prompt_pos[4 * z + jnp.bitwise_xor(2 * x + c, codes)] >= 0
    live = jnp.tile(live.astype(F32).T, (4, 1))
    rows = 4 * patches.shape[1]
    normed, residual = run(
        norm_kernel,
        [jax.ShapeDtypeStruct((rows, D), BF16), jax.ShapeDtypeStruct((half, rows), BF16)],
        [],
        *patch_parts,
        vit_gain.reshape(2, half),
        scalars=where,
        grant=MOST,
    )
    fourth, normed, out_x, out_c, text_second, merge_second, live = fence(
        next_z(third),
        normed,
        over_x(out_held),
        over_c(out_held),
        next_z(text_first),
        merge_second,
        live,
    )
    out_pieces = [out_held, out_x, out_c, over_c(out_x)]
    vit_weight = [sliced, second, third, fourth]
    merge_third = next_z(merge_second)
    attended = run(
        encode_kernel,
        jax.ShapeDtypeStruct((2 * HEAD, rows), BF16),
        [pltpu.VMEM((D, 512), BF16)],
        normed,
        *vit_weight,
        live,
        scalars=where,
    )
    attended, merge_third = fence(attended, merge_third)
    merge_fourth = next_z(merge_third)
    text_third = next_z(text_second)
    pieces = run(
        split_kernel,
        jax.ShapeDtypeStruct((16, dec_qkv.shape[0], dec_qkv.shape[1] // 16), BF16),
        [],
        dec_qkv,
    )
    turned = dec_out.T
    att_y, att_x, att_xy, merge_fourth, text_fourth, pieces, dec_came = fence(
        over_y(attended),
        over_x(attended),
        over_xy(attended),
        merge_fourth,
        next_z(text_third),
        pieces,
        send_out_y(turned),
    )
    head_parts = [attended, att_y, over_c(attended), over_c(att_y), att_x, att_xy]
    head_parts += [over_c(att_x), over_c(att_xy)]
    pieces = lax.all_to_all(pieces, "wide", 0, 0, tiled=True)
    merge_rows = [merge_first, merge_second, merge_third, merge_fourth]
    part = jax.ShapeDtypeStruct((320, 128), F32)
    kept, sent = run(
        merge_kernel,
        [part, part],
        [
            pltpu.VMEM((4, D, 256), BF16),
            pltpu.VMEM((2, half, half), BF16),
            pltpu.VMEM((4,) + merge_first.shape, BF16),
        ],
        *head_parts,
        residual,
        *out_pieces,
        *merge_rows,
        scalars=where,
        grant=MOST,
    )
    stacked = jnp.stack([text_embeds, text_second, text_third, text_fourth])
    kept, sent, pieces, text_y, text_x = fence(
        kept, sent, pieces, over_y(stacked), over_x(stacked)
    )
    came = over_y(sent)
    text_weight, token_weight, token_gain = run(
        weight_kernel,
        [
            jax.ShapeDtypeStruct((D, 384), BF16),
            jax.ShapeDtypeStruct((4, 384, D // 4), BF16),
            jax.ShapeDtypeStruct((4, D // 4, 128), F32),
        ],
        [pltpu.VMEM((4, D // 4, 384), BF16)],
        pieces,
        over_c(pieces),
        dec_gain[None],
        scalars=where,
    )
    merged = (kept + came).astype(BF16)
    merged, text_y, text_x = fence(merged, text_y, text_x)
    sx = jnp.arange(2, dtype=jnp.int32)[:, None, None]
    k = jnp.arange(4, dtype=jnp.int32)[None, :, None]
    sc = jnp.arange(2, dtype=jnp.int32)[None, None, :]
    image = 4 * ((z + 4 - k) % 4) + 2 * (sx ^ x ^ y) + sc
    flat_pos = prompt_pos[image.reshape(-1)].reshape(1, -1)
    select, is_text = run(
        select_kernel,
        [
            jax.ShapeDtypeStruct((8 * text_rows, flat_pos.shape[1]), BF16),
            jax.ShapeDtypeStruct((8 * text_rows, 128), F32),
        ],
        [],
        flat_pos,
        scalars=where,
    )

    def project_text(text_y, text_x, corner):
        return run(
            text_kernel,
            jax.ShapeDtypeStruct((8 * text_rows, 384), BF16),
            [],
            stacked,
            text_y,
            text_x,
            *corner,
            dec_gain.reshape(2, half),
            text_weight,
            is_text,
            scalars=where,
        )

    dec_both = jnp.stack([turned, dec_came])
    *tokens, dec_came = fence(*around_z(merged), send_out_far(dec_both))
    dec_held = jnp.where(z // 2 == y, dec_both, dec_came)
    tokens = jnp.stack(tokens)
    corner = [over_y(text_x[:2]), over_x(text_y[2:])]
    text_proj = project_text(text_y, text_x, corner)
    token_y, token_x, token_xy, text_proj, dec_came = fence(
        over_y(tokens), over_x(tokens), over_xy(tokens), text_proj, send_out_near(dec_held)
    )
    dec_held = jnp.stack([dec_held, dec_came])
    token_parts = [tokens, token_y, over_c(tokens), over_c(token_y)]
    token_parts += [token_x, token_xy, over_c(token_x), over_c(token_xy)]

    lanes = jax.ShapeDtypeStruct((8 * text_rows, 128), BF16)
    query, key, value = run(
        place_kernel,
        [lanes, lanes, lanes],
        [pltpu.VMEM((384, 1024), BF16)],
        *token_parts,
        token_gain,
        token_weight,
        select,
        text_proj,
    )
    heads = run(
        decode_kernel,
        jax.ShapeDtypeStruct((16, 16, text_rows // 16 * HEAD), BF16),
        [],
        query,
        key,
        value,
        over_c(key),
        over_c(value),
        scalars=where,
    )
    heads, dec_x, dec_c = fence(heads, over_x(dec_held), over_c(dec_held))
    by_core = [[2 * w_ + y_ for w_ in range(c_, 16, 2) for y_ in (0, 1)] for c_ in (0, 1)]
    heads = lax.all_to_all(
        heads, ("wide", "narrow"), 0, 0, axis_index_groups=by_core, tiled=True
    )
    routed = run(
        route_kernel,
        jax.ShapeDtypeStruct((4, text_rows, 320), BF16),
        [],
        *token_parts,
        flat_pos,
        scalars=where,
    )
    routed = routed.reshape(4, text_rows, 4, D // 16)
    routed = lax.dynamic_slice_in_dim(routed, 2 * y, 2, axis=2)
    ordered = jnp.stack(
        [
            lax.dynamic_index_in_dim(routed, jnp.bitwise_xor(2 * x + c, code), 0, keepdims=False)
            for code in range(4)
        ]
    )
    ordered = ordered.transpose(1, 2, 0, 3).reshape(text_rows, half)
    mine = w * text_rows + jnp.arange(text_rows, dtype=jnp.int32)
    is_image = jnp.any(mine[:, None] == prompt_pos.reshape(1, -1), axis=1)
    dec_in = jnp.where(is_image[:, None], ordered, text_embeds)
    return run(
        finish_kernel,
        jax.ShapeDtypeStruct(text_embeds.shape, BF16),
        [
            pltpu.VMEM((2, half, half), BF16),
            pltpu.VMEM((2, text_rows, half), BF16),
        ],
        heads,
        dec_held,
        dec_x,
        dec_c,
        over_c(dec_x),
        dec_in,
        scalars=where,
    )


def solution(mesh):
    placed = (
        P("wide", None, "narrow"),
        P("wide", None),
        P(),
        P("wide", "narrow"),
        P("narrow", "wide"),
        P(None, "narrow", "wide"),
        P("wide", "narrow"),
        P(),
        P(),
        P("wide", "narrow"),
        P("narrow", "wide"),
    )
    sizes = (mesh.shape["wide"], mesh.shape["narrow"])
    shards = shards_fast if sizes == (16, 2) else shards_any
    return jax.shard_map(
        shards, mesh=mesh, in_specs=placed, out_specs=P("wide", "narrow"), check_vma=False
    )
```

```python
import jax
import jax.numpy as jnp
from jax import lax
from jax.experimental import pallas as pl
from jax.experimental.pallas import tpu as pltpu
from jax.sharding import PartitionSpec as P

D = 1280
HEAD = 80
PATCH_SIDE = 16


eps_norm = 1e-06


def layer_norm(values, gain):
    center = values - jnp.mean(values, axis=-1, keepdims=True)
    spread = jnp.mean(center * center, axis=-1, keepdims=True)
    return center * lax.rsqrt(spread + eps_norm) * gain


def rms_norm(values, gain):
    return values * lax.rsqrt(jnp.mean(values * values, axis=-1, keepdims=True) + eps_norm) * gain


def add_rows(left, piece):
    return jnp.dot(left, piece, preferred_element_type=jnp.float32)


def image_attention(query, keys, values, keep):
    scores = jnp.einsum(
        "iqhd,ikhd->ihqk", query, keys, preferred_element_type=jnp.float32
    ) * HEAD ** (-0.5)
    scores = jnp.where(keep[:, None, None, :], scores, -jnp.inf)
    weights = jnp.exp(scores - jnp.max(scores, axis=-1, keepdims=True))
    total = jnp.sum(weights, axis=-1)
    mixed = jnp.einsum(
        "ihqk,ikhd->iqhd", weights.astype(jnp.bfloat16), values, preferred_element_type=jnp.float32
    )
    return (mixed / jnp.transpose(total, (0, 2, 1))[..., None]).astype(jnp.bfloat16)


def attend(state, query, query_pos, keys, values, key_pos):
    best, total, summed = state
    scores = jnp.einsum("qhd,khd->hqk", query, keys, preferred_element_type=jnp.float32) * HEAD ** (
        -0.5
    )
    allowed = key_pos[None, :] <= query_pos[:, None]
    scores = jnp.where(allowed[None], scores, -jnp.inf)
    new_best = jnp.maximum(best, jnp.max(scores, axis=-1))
    shift = jnp.where(jnp.isfinite(new_best), new_best, 0.0)
    weights = jnp.exp(scores - shift[..., None])
    fade = jnp.exp(best - shift)
    total = total * fade + jnp.sum(weights, axis=-1)
    update = jnp.einsum(
        "hqk,khd->hqd", weights.astype(jnp.bfloat16), values, preferred_element_type=jnp.float32
    )
    summed = summed * fade[..., None] + update
    return (new_best, total, summed)


def fresh_state(heads, count):
    return (
        jnp.full((heads, count), -jnp.inf, jnp.float32),
        jnp.zeros((heads, count), jnp.float32),
        jnp.zeros((heads, count, HEAD), jnp.float32),
    )


def finish(state):
    best, total, summed = state
    return summed / total[..., None]


def shards_any(
    patches,
    grid,
    vit_gain,
    vit_qkv,
    vit_out,
    merge_weight,
    text_embeds,
    prompt_pos,
    dec_gain,
    dec_qkv,
    dec_out,
):
    images, slots, part_width = patches.shape
    side = PATCH_SIDE
    half_side = side // 2
    rows_vit = images * slots
    local_heads = vit_qkv.shape[1] // (3 * HEAD)
    whole = lax.all_gather(patches, "narrow", axis=2, tiled=True)
    normed = (
        layer_norm(whole.astype(jnp.float32), vit_gain).astype(jnp.bfloat16).reshape(rows_vit, D)
    )
    projected = add_rows(normed, lax.all_gather(vit_qkv, "wide", axis=0, tiled=True))
    projected = projected.astype(jnp.bfloat16).reshape(images, slots, local_heads, 3, HEAD)
    slot_ids = jnp.arange(slots, dtype=jnp.int32)
    keep = ((slot_ids // side)[None, :] < grid[:, 0:1]) & (
        (slot_ids % side)[None, :] < grid[:, 1:2]
    )
    attended = image_attention(
        projected[:, :, :, 0], projected[:, :, :, 1], projected[:, :, :, 2], keep
    )
    attended = attended.reshape(rows_vit, local_heads * HEAD)
    vit_partial = jnp.dot(
        attended,
        lax.all_gather(vit_out, "wide", axis=1, tiled=True),
        preferred_element_type=jnp.float32,
    )
    vit_branch = lax.psum_scatter(vit_partial, "narrow", scatter_dimension=1, tiled=True)
    after = (patches.reshape(rows_vit, part_width).astype(jnp.float32) + vit_branch).astype(
        jnp.bfloat16
    )
    grouped = after.reshape(images, half_side, 2, half_side, 2, part_width).transpose(
        0, 1, 3, 2, 4, 5
    )
    grouped = grouped.reshape(images * half_side * half_side, 4 * part_width)
    piece = lax.all_gather(merge_weight, "wide", axis=2, tiled=True)
    flat_piece = piece.reshape(4 * part_width, piece.shape[2])
    merge_partial = jnp.dot(grouped, flat_piece, preferred_element_type=jnp.float32)
    merged = lax.psum_scatter(merge_partial, "narrow", scatter_dimension=1, tiled=True).astype(
        jnp.bfloat16
    )
    text_rows = text_embeds.shape[0]
    half_rows = text_rows // 2
    wide_index = lax.axis_index("wide")
    offsets = jnp.arange(text_rows, dtype=jnp.int32)
    mine = wide_index * text_rows + offsets
    flat_pos = prompt_pos.reshape(-1)
    select = (mine[:, None] == flat_pos[None, :]).astype(jnp.bfloat16)
    routed = jnp.dot(
        select,
        lax.all_gather(merged, "wide", axis=0, tiled=True),
        preferred_element_type=jnp.float32,
    )
    is_image = jnp.any(mine[:, None] == flat_pos[None, :], axis=1)
    dec_in = jnp.where(is_image[:, None], routed.astype(jnp.bfloat16), text_embeds)
    dec_whole = lax.all_gather(dec_in, "narrow", axis=1, tiled=True)
    dec_normed = rms_norm(dec_whole.astype(jnp.float32), dec_gain).astype(jnp.bfloat16)
    dec_proj = add_rows(dec_normed, lax.all_gather(dec_qkv, "wide", axis=0, tiled=True))
    dec_proj = dec_proj.astype(jnp.bfloat16).reshape(text_rows, local_heads, 3, HEAD)
    queries = dec_proj[:, :, 0]
    keys = dec_proj[:, :, 1].reshape(text_rows, local_heads * HEAD)
    values = dec_proj[:, :, 2].reshape(text_rows, local_heads * HEAD)
    low_pos = mine[:half_rows]
    high_pos = mine[half_rows:]
    low_query = queries[:half_rows]
    high_query = queries[half_rows:]
    start_state = (
        fresh_state(local_heads, half_rows),
        fresh_state(local_heads, text_rows - half_rows),
    )
    key_piece = lax.all_gather(keys, "wide", axis=0, tiled=True)
    value_piece = lax.all_gather(values, "wide", axis=0, tiled=True)
    count = key_piece.shape[0]
    span_rows = count
    while span_rows > 2048 and span_rows % 2 == 0:
        span_rows = span_rows // 2
    key_heads = key_piece.reshape(count, local_heads, HEAD)
    value_heads = value_piece.reshape(count, local_heads, HEAD)

    def one_span(index, carry):
        begin = (index * span_rows).astype(jnp.int32)
        key_span = lax.dynamic_slice_in_dim(key_heads, begin, span_rows)
        value_span = lax.dynamic_slice_in_dim(value_heads, begin, span_rows)
        key_pos = begin + jnp.arange(span_rows, dtype=jnp.int32)
        earliest = jnp.min(key_pos)
        first = lax.cond(
            earliest <= jnp.max(low_pos),
            lambda inner: attend(inner, low_query, low_pos, key_span, value_span, key_pos),
            lambda inner: inner,
            carry[0],
        )
        second = lax.cond(
            earliest <= jnp.max(high_pos),
            lambda inner: attend(inner, high_query, high_pos, key_span, value_span, key_pos),
            lambda inner: inner,
            carry[1],
        )
        return (first, second)

    final = lax.fori_loop(0, count // span_rows, one_span, start_state)
    heads_out = jnp.concatenate([finish(final[0]), finish(final[1])], axis=1)
    heads_out = (
        heads_out.transpose(1, 0, 2).reshape(text_rows, local_heads * HEAD).astype(jnp.bfloat16)
    )
    dec_partial = jnp.dot(
        heads_out,
        lax.all_gather(dec_out, "wide", axis=1, tiled=True),
        preferred_element_type=jnp.float32,
    )
    dec_branch = lax.psum_scatter(
        dec_partial.astype(jnp.bfloat16), "narrow", scatter_dimension=1, tiled=True
    ).astype(jnp.float32)
    result = (dec_in.astype(jnp.float32) + dec_branch).astype(jnp.bfloat16)
    return result


CROSS_X = [(w, w ^ 2) for w in range(16)]
CROSS_C = [(w, w ^ 1) for w in range(16)]
CROSS_Y = [(0, 1), (1, 0)]
GROUPS_Z = [[b, 4 + b, 8 + b, 12 + b] for b in range(4)]
GROUPS_B = [[4 * z + b for b in range(4)] for z in range(4)]
FOUR = ((0, 0), (0, 1), (1, 0), (1, 1))
SMEM = pl.BlockSpec(memory_space=pltpu.SMEM)
F32 = jnp.float32
BF16 = jnp.bfloat16
GRANT = 48 * 1024 * 1024
MOST = 59 * 1024 * 1024


def over_x(value):
    return lax.ppermute(value, "wide", CROSS_X)


def over_c(value):
    return lax.ppermute(value, "wide", CROSS_C)


def over_y(value):
    return lax.ppermute(value, "narrow", CROSS_Y)


RING_Z = [(4 * a + b, 4 * n + b) for a, n in ((0, 1), (1, 3), (3, 2), (2, 0)) for b in range(4)]


def next_z(value):
    return lax.ppermute(value, "wide", RING_Z)


def z_behind(z, steps):
    place = lax.rem(jnp.bitwise_xor(z, z // 2) + 4 - steps, 4)
    return jnp.bitwise_xor(place, place // 2)


def around_z(value):
    return [value] + [
        lax.ppermute(value, "wide", [(w, (w + 4 * k) % 16) for w in range(16)]) for k in (1, 2, 3)
    ]


def over_xy(value):
    both = [(2 * w + y, 2 * (w ^ 2) + 1 - y) for w in range(16) for y in (0, 1)]
    return lax.ppermute(value, ("wide", "narrow"), both)


def share_xy(value):
    return [[value, over_y(value)], [over_x(value), over_xy(value)]]


def share_xyc(value):
    pieces = share_xy(value)
    return [
        over_c(pieces[ex][ey]) if ec else pieces[ex][ey]
        for ex, ec in FOUR
        for ey in (0, 1)
    ]


def contract(left, right, left_dim, right_dim):
    return lax.dot_general(
        left, right, (((left_dim,), (right_dim,)), ((), ())), preferred_element_type=F32
    )


def patch_order():
    row = lax.broadcasted_iota(jnp.int32, (256, 256), 0)
    column = lax.broadcasted_iota(jnp.int32, (256, 256), 1)
    sub, token = row // 64, row % 64
    source = (2 * (token // 8) + sub // 2) * 16 + 2 * (token % 8) + sub % 2
    return jnp.where(column == source, 1.0, 0.0).astype(BF16)


def norm_kernel(where, *refs):
    parts = refs[:8]
    gain, normed, residual = refs[8:]
    order = patch_order()
    own_gain = gain[pl.ds(where[3], 1), :]
    other_gain = gain[pl.ds(1 - where[3], 1), :]
    for slot in range(4):
        raw = parts[2 * slot][...]
        own = raw.astype(F32)
        other = parts[2 * slot + 1][...].astype(F32)
        mean = (
            jnp.sum(own, axis=-1, keepdims=True) + jnp.sum(other, axis=-1, keepdims=True)
        ) * (1.0 / D)
        own = own - mean
        other = other - mean
        spread = (
            jnp.sum(own * own, axis=-1, keepdims=True)
            + jnp.sum(other * other, axis=-1, keepdims=True)
        ) * (1.0 / D)
        scale = lax.rsqrt(spread + eps_norm)
        own = (own * scale * own_gain).astype(BF16)
        other = (other * scale * other_gain).astype(BF16)
        at = slice(slot * 256, (slot + 1) * 256)
        normed[at, : D // 2] = contract(order, own, 1, 0).astype(BF16)
        normed[at, D // 2 :] = contract(order, other, 1, 0).astype(BF16)
        residual[:, at] = contract(raw, order, 0, 1).astype(BF16)


def own_half_first(where, block):
    row = block * (D // 16) - where[3] * (D // 2)
    return pl.multiple_of(jnp.where(row < 0, row + D, row), 16)


def encode_kernel(where, normed, first, second, third, fourth, keep, out, weight):
    block = D // 16
    here = where[1] * 2 + where[2]
    for steps, piece in enumerate((first, second, third, fourth)):
        z = z_behind(where[0], steps)
        for code in range(4):
            row = own_half_first(where, 4 * z + jnp.bitwise_xor(here, code))
            weight[pl.ds(row, block), :] = piece[code * block : (code + 1) * block, :]
    for slot in range(4):
        proj = contract(normed[slot * 256 : (slot + 1) * 256, :], weight[...], 1, 0).astype(BF16)
        live = keep[:, slot : slot + 1] > 0.0
        for head in (0, 1):
            base = head * 3 * HEAD
            query = proj[:, base : base + HEAD]
            key_rows = proj[:, base + HEAD : base + 2 * HEAD]
            value_rows = proj[:, base + 2 * HEAD : base + 3 * HEAD]
            scores = contract(key_rows, query, 1, 1) * HEAD ** (-0.5)
            scores = jnp.where(live, scores, -jnp.inf)
            weights = jnp.exp(scores - jnp.max(scores, axis=0, keepdims=True))
            total = jnp.sum(weights, axis=0, keepdims=True)
            mixed = contract(value_rows, weights.astype(BF16), 0, 0)
            out[head * HEAD : (head + 1) * HEAD, slot * 256 : (slot + 1) * 256] = (
                mixed / total
            ).astype(BF16)


def fill_out_weight(where, pieces, weight):
    here = lax.rem(where[0], 2) * 4 + where[1] * 2 + where[2]
    block = D // 16
    for code, piece in zip((0, 2, 1, 3), pieces):
        for ez in (0, 1):
            row = jnp.bitwise_xor(here, 4 * ez + code) * block
            for part in (0, 1):
                weight[part, pl.ds(pl.multiple_of(row, 16), block), :] = piece[ez, part]


def merge_kernel(where, *refs):
    parts = refs[:8]
    residual, out_pieces, arrived = refs[8], refs[9:13], refs[13:17]
    keep_out, send_out, heads, out_weight, weight = refs[17:]
    here = where[1] * 2 + where[2]
    fill_out_weight(where, out_pieces, out_weight)
    for code in range(4):
        for ey in (0, 1):
            base = ey * (D // 2) + 2 * HEAD * jnp.bitwise_xor(here, code)
            rows = pl.ds(pl.multiple_of(base, 16), 2 * HEAD)
            for slot in range(4):
                at = (slot ^ code) * 256
                heads[slot, rows, :] = parts[2 * code + ey][:, at : at + 256]
    for steps in range(4):
        weight[z_behind(where[0], steps)] = arrived[steps][...]
    sub_rows = [[], [], [], []]
    for slot in range(4):
        at = slice(slot * 256, (slot + 1) * 256)
        branch = contract(out_weight[0], heads[slot, : D // 2, :], 1, 0) + contract(
            out_weight[1], heads[slot, D // 2 :, :], 1, 0
        )
        after = (residual[:, at].astype(F32) + branch).astype(BF16)
        for sub in range(4):
            sub_rows[sub].append(after[:, sub * 64 : (sub + 1) * 64])
    total = 0.0
    for sub in range(4):
        left = jnp.concatenate([weight[z, sub] for z in range(4)], axis=0)
        total = total + contract(left, jnp.concatenate(sub_rows[sub], axis=1), 1, 0)
    low, high = total[:, :128], total[:, 128:]

    def by_core(value):
        turned = jnp.concatenate([value[:, 64:], value[:, :64]], axis=1)
        return jnp.where(where[2] == 0, value, turned)

    keep_out[...] = by_core(jnp.where(where[3] == 0, low, high))
    send_out[...] = by_core(jnp.where(where[3] == 0, high, low))


def split_kernel(whole, out):
    count = whole.shape[1] // 16
    for at in range(16):
        out[at] = whole[:, at * count : (at + 1) * count]


def weight_kernel(where, own, other, gain, text_weight, token_weight, token_gain, rows):
    block = D // 16
    zeros = jnp.zeros((block, 128 - HEAD), BF16)
    here = where[1] * 2 + where[2]
    for at in range(16):
        low = jnp.where(where[2] == 0, own[at].astype(F32), other[at].astype(F32))
        high = jnp.where(where[2] == 0, other[at].astype(F32), own[at].astype(F32))
        piece = jnp.concatenate([low, high], axis=1).astype(BF16)
        padded = jnp.concatenate(
            [part for k in range(3) for part in (piece[:, k * HEAD : (k + 1) * HEAD], zeros)],
            axis=1,
        )
        text_weight[pl.ds(own_half_first(where, at), block), :] = padded
        z = at // 4
        code = jnp.bitwise_xor(here, at % 4)
        rows[code, z * block : (z + 1) * block, :] = padded
        column = jnp.broadcast_to(gain[:, at * block : (at + 1) * block], (128, block)).T
        token_gain[code, z * block : (z + 1) * block, :] = column
    for code in range(4):
        token_weight[code] = rows[code].T


def text_kernel(where, own, own_y, own_x, corner_low, corner_high, gain, weight, is_text, out):
    own_gain = gain[pl.ds(where[3], 1), :]
    other_gain = gain[pl.ds(1 - where[3], 1), :]
    count = own.shape[1]
    for steps in range(4):
        corner = (corner_low, corner_high)[steps // 2][steps % 2]
        for ex in (0, 1):
            left = (own, own_x)[ex][steps].astype(F32)
            right = (corner if ex else own_y[steps]).astype(F32)
            squares = jnp.sum(left * left, axis=-1, keepdims=True) + jnp.sum(
                right * right, axis=-1, keepdims=True
            )
            scale = lax.rsqrt(squares * (1.0 / D) + eps_norm)
            left = (left * scale * own_gain).astype(BF16)
            right = (right * scale * other_gain).astype(BF16)
            proj = contract(left, weight[: D // 2, :], 1, 0) + contract(
                right, weight[D // 2 :, :], 1, 0
            )
            row = (2 * z_behind(where[0], steps) + jnp.bitwise_xor(where[1], ex)) * count
            at = pl.ds(pl.multiple_of(row, 16), count)
            out[at, :] = jnp.where(is_text[at, :1] > 0.0, proj, 0.0).astype(BF16)


def select_kernel(where, flat_pos, select, is_text):
    positions = flat_pos[...]
    block_rows = select.shape[0] // 8
    for block in range(8):
        first = (2 * block + where[2]) * block_rows
        row = first + lax.broadcasted_iota(jnp.int32, (block_rows, positions.shape[1]), 0)
        hit = jnp.where(row == positions, 1.0, 0.0)
        at = slice(block * block_rows, (block + 1) * block_rows)
        select[at, :] = hit.astype(BF16)
        none = 1.0 - jnp.max(hit, axis=-1, keepdims=True)
        is_text[at, :] = jnp.broadcast_to(none, (block_rows, 128))


def token_columns(parts, sx):
    blocks = []
    for code, (ex, _) in enumerate(FOUR):
        part = parts[2 * code + (sx ^ ex)]
        blocks.append(jnp.concatenate([part[z] for z in range(4)], axis=1))
    return blocks


def place_kernel(*refs):
    parts = refs[:8]
    gain, weight, select, text_proj, query, key_out, value_out, proj = refs[8:]
    for sx in (0, 1):
        blocks = token_columns(parts, sx)
        squares = sum(
            jnp.sum(jnp.square(block.astype(F32)), axis=0, keepdims=True) for block in blocks
        )
        scale = lax.rsqrt(squares * (1.0 / D) + eps_norm)
        total = 0.0
        for at, block in enumerate(blocks):
            normed = (block.astype(F32) * scale * gain[at][:, :1]).astype(BF16)
            total = total + contract(weight[at], normed, 1, 0)
        proj[:, sx * 512 : (sx + 1) * 512] = total.astype(BF16)
    rows = contract(select[...], proj[...], 1, 1) + text_proj[...].astype(F32)
    rows = rows.astype(BF16)
    query[...] = rows[:, :128]
    key_out[...] = rows[:, 128:256]
    value_out[...] = rows[:, 256:]


def route_kernel(where, *refs):
    parts = refs[:8]
    flat_pos, routed = refs[8:]
    positions = flat_pos[...]
    block_rows = routed.shape[1]
    own_block = 4 * where[0] + 2 * where[1] + where[2]
    row = own_block * block_rows + lax.broadcasted_iota(
        jnp.int32, (block_rows, positions.shape[1]), 0
    )
    select = jnp.where(row == positions, 1.0, 0.0).astype(BF16)
    low, high = token_columns(parts, 0), token_columns(parts, 1)
    for at in range(4):
        moved = contract(select[:, :512], low[at], 1, 1) + contract(
            select[:, 512:], high[at], 1, 1
        )
        routed[at] = moved.astype(BF16)


def decode_kernel(where, query, own_key, own_value, other_key, other_value, out):
    rows = query.shape[0] // 8
    later = where[2] > 0
    for block in range(8):
        count = (block + 1) * rows
        asked = query[block * rows : count, :]
        own = contract(asked, own_key[:count, :], 1, 1) * HEAD ** (-0.5)
        other = contract(asked, other_key[:count, :], 1, 1) * HEAD ** (-0.5)
        row = lax.broadcasted_iota(jnp.int32, (rows, count), 0) + block * rows
        column = lax.broadcasted_iota(jnp.int32, (rows, count), 1)
        own = jnp.where(column <= row, own, -jnp.inf)
        limit = jnp.where(later, count, block * rows)
        other = jnp.where(column < limit, other, -jnp.inf)
        best = jnp.maximum(
            jnp.max(own, axis=-1, keepdims=True), jnp.max(other, axis=-1, keepdims=True)
        )
        own = jnp.exp(own - best)
        other = jnp.exp(other - best)
        total = jnp.sum(own, axis=-1, keepdims=True) + jnp.sum(other, axis=-1, keepdims=True)
        mixed = contract(own.astype(BF16), own_value[:count, :], 1, 0) + contract(
            other.astype(BF16), other_value[:count, :], 1, 0
        )
        mixed = (mixed / total).astype(BF16)
        for group in range(rows // 16):
            piece = mixed[group * 16 : (group + 1) * 16, :HEAD]
            for y in (0, 1):
                out[2 * block + y, :, group * HEAD : (group + 1) * HEAD] = piece


def finish_kernel(where, heads, own, at_x, at_c, at_xc, residual, out, weight, sorted_heads):
    fill_out_weight(where, (own, at_x, at_c, at_xc), weight)
    for at in range(16):
        chip, y = at // 2, at % 2
        half = jnp.bitwise_xor(where[3], y)
        for group in range(out.shape[0] // 16):
            sorted_heads[
                half, group * 16 : (group + 1) * 16, chip * HEAD : (chip + 1) * HEAD
            ] = heads[at, :, group * HEAD : (group + 1) * HEAD]
    branch = contract(sorted_heads[0], weight[0], 1, 1) + contract(sorted_heads[1], weight[1], 1, 1)
    out[...] = (residual[...].astype(F32) + branch).astype(BF16)


def run(kernel, shapes, scratch, *operands, scalars=None, grant=GRANT):
    specs = [pl.BlockSpec()] * len(operands)
    if scalars is not None:
        specs, operands = [SMEM] + specs, (scalars,) + operands
    single = not isinstance(shapes, (list, tuple))
    return pl.pallas_call(
        kernel,
        out_shape=shapes,
        in_specs=specs,
        out_specs=pl.BlockSpec() if single else [pl.BlockSpec()] * len(shapes),
        scratch_shapes=scratch,
        compiler_params=pltpu.CompilerParams(vmem_limit_bytes=grant),
    )(*operands)


OUT_Y = [(2 * w + 1 - w // 8, 2 * w + w // 8) for w in range(16)]
OUT_FAR = [(2 * w + w // 8, 2 * (w ^ 8) + w // 8) for w in range(16)]
OUT_NEAR = [(w, w ^ 4) for w in range(16)]


def send_out_y(turned):
    return lax.ppermute(turned, ("wide", "narrow"), OUT_Y)


def send_out_far(both):
    return lax.ppermute(both, ("wide", "narrow"), OUT_FAR)


def send_out_near(held):
    return lax.ppermute(held, "wide", OUT_NEAR)


def out_over_y(turned):
    return jnp.stack([turned, send_out_y(turned)])


def out_over_far(both, z, y):
    return jnp.where(z // 2 == y, both, send_out_far(both))


def out_over_near(held):
    return jnp.stack([held, send_out_near(held)])


def fence(*values):
    return lax.optimization_barrier(values)


def shards_fast(
    patches,
    grid,
    vit_gain,
    vit_qkv,
    vit_out,
    merge_weight,
    text_embeds,
    prompt_pos,
    dec_gain,
    dec_qkv,
    dec_out,
):
    w = lax.axis_index("wide").astype(jnp.int32)
    y = lax.axis_index("narrow").astype(jnp.int32)
    z, x, c = w // 4, (w // 2) % 2, w % 2
    where = jnp.stack([z, x, c, y])
    half = D // 2
    text_rows = text_embeds.shape[0]

    columns = vit_qkv.shape[1] // 4
    sliced = vit_qkv.reshape(-1, 2, 2, columns).transpose(1, 2, 0, 3)
    sliced = jnp.pad(sliced, ((0, 0), (0, 0), (0, 0), (0, 512 - columns)))

    def halves(value, bit):
        own = lax.dynamic_index_in_dim(value, bit, 0, keepdims=False)
        return own, lax.dynamic_index_in_dim(value, 1 - bit, 0, keepdims=False)

    own_cols, sent_cols = halves(sliced, x)
    merge_first = merge_weight.transpose(0, 2, 1)
    patch, sent_cols = fence(patches[0], sent_cols)
    came_cols, patch_y, merge_second, out_held, text_second = fence(
        over_x(sent_cols),
        over_y(patch),
        next_z(merge_first),
        out_over_y(vit_out.T),
        next_z(text_embeds),
    )
    own_cols, sent_cols = halves(jnp.stack([own_cols, came_cols], axis=-3), c)
    patch, sent_cols = fence(patch, sent_cols)
    sliced = jnp.stack([own_cols, over_c(sent_cols)], axis=-3).reshape(-1, 512)
    second, patch_x, out_held = fence(
        next_z(sliced), over_x(patch), out_over_far(out_held, z, y)
    )
    patch_xy = over_xy(patch)
    third, patch_xy, out_held, text_second = fence(
        next_z(second), patch_xy, out_over_near(out_held), text_second
    )
    patch_parts = [patch, patch_y, over_c(patch), over_c(patch_y), patch_x, patch_xy]
    patch_parts += [over_c(patch_x), over_c(patch_xy)]
    codes = jnp.arange(4, dtype=jnp.int32)
    live = prompt_pos[4 * z + jnp.bitwise_xor(2 * x + c, codes)] >= 0
    live = jnp.tile(live.astype(F32).T, (4, 1))
    rows = 4 * patches.shape[1]
    normed, residual = run(
        norm_kernel,
        [jax.ShapeDtypeStruct((rows, D), BF16), jax.ShapeDtypeStruct((half, rows), BF16)],
        [],
        *patch_parts,
        vit_gain.reshape(2, half),
        scalars=where,
        grant=MOST,
    )
    fourth, normed, out_x, out_c, text_second, merge_second, live = fence(
        next_z(third),
        normed,
        over_x(out_held),
        over_c(out_held),
        text_second,
        merge_second,
        live,
    )
    out_pieces = [out_held, out_x, out_c, over_c(out_x)]
    vit_weight = [sliced, second, third, fourth]
    merge_third = next_z(merge_second)
    attended = run(
        encode_kernel,
        jax.ShapeDtypeStruct((2 * HEAD, rows), BF16),
        [pltpu.VMEM((D, 512), BF16)],
        normed,
        *vit_weight,
        live,
        scalars=where,
    )
    attended, merge_third = fence(attended, merge_third)
    merge_fourth = next_z(merge_third)
    text_third = next_z(text_second)
    pieces = run(
        split_kernel,
        jax.ShapeDtypeStruct((16, dec_qkv.shape[0], dec_qkv.shape[1] // 16), BF16),
        [],
        dec_qkv,
    )
    turned = dec_out.T
    att_y, att_x, att_xy, merge_fourth, text_fourth, pieces, dec_came = fence(
        over_y(attended),
        over_x(attended),
        over_xy(attended),
        merge_fourth,
        next_z(text_third),
        pieces,
        send_out_y(turned),
    )
    head_parts = [attended, att_y, over_c(attended), over_c(att_y), att_x, att_xy]
    head_parts += [over_c(att_x), over_c(att_xy)]
    pieces = lax.all_to_all(pieces, "wide", 0, 0, tiled=True)
    merge_rows = [merge_first, merge_second, merge_third, merge_fourth]
    part = jax.ShapeDtypeStruct((320, 128), F32)
    kept, sent = run(
        merge_kernel,
        [part, part],
        [
            pltpu.VMEM((4, D, 256), BF16),
            pltpu.VMEM((2, half, half), BF16),
            pltpu.VMEM((4,) + merge_first.shape, BF16),
        ],
        *head_parts,
        residual,
        *out_pieces,
        *merge_rows,
        scalars=where,
        grant=MOST,
    )
    stacked = jnp.stack([text_embeds, text_second, text_third, text_fourth])
    kept, sent, pieces, text_y, text_x = fence(
        kept, sent, pieces, over_y(stacked), over_x(stacked)
    )
    came = over_y(sent)
    text_weight, token_weight, token_gain = run(
        weight_kernel,
        [
            jax.ShapeDtypeStruct((D, 384), BF16),
            jax.ShapeDtypeStruct((4, 384, D // 4), BF16),
            jax.ShapeDtypeStruct((4, D // 4, 128), F32),
        ],
        [pltpu.VMEM((4, D // 4, 384), BF16)],
        pieces,
        over_c(pieces),
        dec_gain[None],
        scalars=where,
    )
    merged = (kept + came).astype(BF16)
    merged, text_y, text_x = fence(merged, text_y, text_x)
    sx = jnp.arange(2, dtype=jnp.int32)[:, None, None]
    k = jnp.arange(4, dtype=jnp.int32)[None, :, None]
    sc = jnp.arange(2, dtype=jnp.int32)[None, None, :]
    image = 4 * ((z + 4 - k) % 4) + 2 * (sx ^ x ^ y) + sc
    flat_pos = prompt_pos[image.reshape(-1)].reshape(1, -1)
    select, is_text = run(
        select_kernel,
        [
            jax.ShapeDtypeStruct((8 * text_rows, flat_pos.shape[1]), BF16),
            jax.ShapeDtypeStruct((8 * text_rows, 128), F32),
        ],
        [],
        flat_pos,
        scalars=where,
    )

    def project_text(text_y, text_x, corner):
        return run(
            text_kernel,
            jax.ShapeDtypeStruct((8 * text_rows, 384), BF16),
            [],
            stacked,
            text_y,
            text_x,
            *corner,
            dec_gain.reshape(2, half),
            text_weight,
            is_text,
            scalars=where,
        )

    dec_both = jnp.stack([turned, dec_came])
    *tokens, dec_came = fence(*around_z(merged), send_out_far(dec_both))
    dec_held = jnp.where(z // 2 == y, dec_both, dec_came)
    tokens = jnp.stack(tokens)
    corner = [over_y(text_x[:2]), over_x(text_y[2:])]
    text_proj = project_text(text_y, text_x, corner)
    token_y, token_x, token_xy, text_proj, dec_came = fence(
        over_y(tokens), over_x(tokens), over_xy(tokens), text_proj, send_out_near(dec_held)
    )
    dec_held = jnp.stack([dec_held, dec_came])
    token_parts = [tokens, token_y, over_c(tokens), over_c(token_y)]
    token_parts += [token_x, token_xy, over_c(token_x), over_c(token_xy)]

    lanes = jax.ShapeDtypeStruct((8 * text_rows, 128), BF16)
    query, key, value = run(
        place_kernel,
        [lanes, lanes, lanes],
        [pltpu.VMEM((384, 1024), BF16)],
        *token_parts,
        token_gain,
        token_weight,
        select,
        text_proj,
    )
    heads = run(
        decode_kernel,
        jax.ShapeDtypeStruct((16, 16, text_rows // 16 * HEAD), BF16),
        [],
        query,
        key,
        value,
        over_c(key),
        over_c(value),
        scalars=where,
    )
    heads, dec_x, dec_c = fence(heads, over_x(dec_held), over_c(dec_held))
    by_core = [[2 * w_ + y_ for w_ in range(c_, 16, 2) for y_ in (0, 1)] for c_ in (0, 1)]
    heads = lax.all_to_all(
        heads, ("wide", "narrow"), 0, 0, axis_index_groups=by_core, tiled=True
    )
    routed = run(
        route_kernel,
        jax.ShapeDtypeStruct((4, text_rows, 320), BF16),
        [],
        *token_parts,
        flat_pos,
        scalars=where,
    )
    routed = routed.reshape(4, text_rows, 4, D // 16)
    routed = lax.dynamic_slice_in_dim(routed, 2 * y, 2, axis=2)
    ordered = jnp.stack(
        [
            lax.dynamic_index_in_dim(routed, jnp.bitwise_xor(2 * x + c, code), 0, keepdims=False)
            for code in range(4)
        ]
    )
    ordered = ordered.transpose(1, 2, 0, 3).reshape(text_rows, half)
    mine = w * text_rows + jnp.arange(text_rows, dtype=jnp.int32)
    is_image = jnp.any(mine[:, None] == prompt_pos.reshape(1, -1), axis=1)
    dec_in = jnp.where(is_image[:, None], ordered, text_embeds)
    return run(
        finish_kernel,
        jax.ShapeDtypeStruct(text_embeds.shape, BF16),
        [
            pltpu.VMEM((2, half, half), BF16),
            pltpu.VMEM((2, text_rows, half), BF16),
        ],
        heads,
        dec_held,
        dec_x,
        dec_c,
        over_c(dec_x),
        dec_in,
        scalars=where,
    )


def solution(mesh):
    placed = (
        P("wide", None, "narrow"),
        P("wide", None),
        P(),
        P("wide", "narrow"),
        P("narrow", "wide"),
        P(None, "narrow", "wide"),
        P("wide", "narrow"),
        P(),
        P(),
        P("wide", "narrow"),
        P("narrow", "wide"),
    )
    sizes = (mesh.shape["wide"], mesh.shape["narrow"])
    shards = shards_fast if sizes == (16, 2) else shards_any
    return jax.shard_map(
        shards, mesh=mesh, in_specs=placed, out_specs=P("wide", "narrow"), check_vma=False
    )
```
